32 devices in a mesh: sec: 4 (over y, core), row: 8 (over z, x).
Axes of the slice: x: 2, y: 2, z: 4, core: 2. Of those that a mesh axis runs over, the one named last changes fastest.
Arguments:
- env_in: bfloat16 [32, 4, 2, 256, 512], P('row', 'sec'), may hold values from -6 to 6
- ket_mps: bfloat16 [4, 4, 2, 512, 512], P(None, 'sec'), may hold values from -0.25 to 0.25
- bra_mps: bfloat16 [4, 4, 2, 256, 256], P(None, 'sec'), may hold values from -0.375 to 0.375
- ket_sizes: int32 [4, 2], replicated, may hold values from 64 to 512, as said below
- bra_sizes: int32 [4, 2], replicated, may hold values from 64 to 256, as said below
- entries: int32 [32, 8, 3], P('row'), may hold values from 0 to 31, as said below
- coeffs: float32 [32, 8], P('row'), may hold values from -3 to 3
Outputs:
- env_out: bfloat16 [32, 4, 2, 256, 512], P('row', 'sec')
The draws below stay inside these ranges and needn't reach their ends.
Inputs may be any that keep to these rules, and one draw needn't show every extreme that they name: `ket_sizes`: each ket sector size is at least 64 and at most 512; one sector has exactly 512. `bra_sizes`: each bra sector size is at least 64 and at most 256; one sector has exactly 256. `entries`: every entry (wo, sp, s) of input channel wi conserves charge: c(wo) = c(wi) + n(sp) - n(s); sp and s lie in 0 to 3.
All inputs are finite; a program needn't handle non-finite values.
Results may differ from the reference program's by a relative error of at most 0.014.
Values may be sent and summed in bfloat16 or wider, within the bound.
A program may use at most 128 MiB of HBM per device.

```python
import jax
import jax.numpy as jnp
from jax import lax

MW = 32
KB = 512
BB = 256
PHYS = 4
EPW = 8
QB = 2
QA = 4
CH = 4
N_ROW = 8


def draw_sizes(key, low, high):
    values = jax.random.randint(key, (QA, QB), low, high + 1)
    where_top = jax.random.randint(jax.random.fold_in(key, 7), (), 0, QA * QB)
    flat = values.reshape(-1)
    flat = jnp.where(jnp.arange(QA * QB) == where_top, high, flat)
    return flat.reshape(QA, QB).astype(jnp.int32)


def draw_ket_sizes(key, part):
    return draw_sizes(jax.random.fold_in(key, 11), KB // 8, KB)


def draw_bra_sizes(key, part):
    return draw_sizes(jax.random.fold_in(key, 13), BB // 4, BB)


def draw_entries(key, part):
    first, second, third = jax.random.split(jax.random.fold_in(key, 17), 3)
    phys_bra = jax.random.randint(first, (MW, EPW), 0, 4)
    phys_try = jax.random.randint(second, (MW, EPW), 0, 4)
    channel = jnp.arange(MW)[:, None]
    klass = channel % 9
    in_a = klass % 3 - 1
    in_b = klass // 3 - 1
    need_a = in_a + phys_bra % 2 - phys_try % 2
    need_b = in_b + phys_bra // 2 - phys_try // 2
    usable = (jnp.abs(need_a) <= 1) & (jnp.abs(need_b) <= 1)
    phys_ket = jnp.where(usable, phys_try, phys_bra)
    need_a = jnp.where(usable, need_a, in_a)
    need_b = jnp.where(usable, need_b, in_b)
    target = need_a + 1 + 3 * (need_b + 1)
    members = (MW - target + 8) // 9
    slots = jnp.arange(EPW)[None, :]
    offset = jax.random.randint(third, (MW, 1), 0, 1 << 20)
    pick = (offset + slots) % members
    out_w = target + 9 * pick
    return jnp.stack([out_w, phys_bra, phys_ket], axis=-1).astype(jnp.int32)


def levels(stream_key, dims, shards, least, high):
    level, own = 1.0, jax.random.fold_in(stream_key, 6)
    for axis_at, parts in shards:
        draws = jnp.exp(jax.random.uniform(jax.random.fold_in(own, axis_at), (parts,), jnp.float32, least / len(shards), high / len(shards)))
        level = level * jnp.repeat(draws, dims[axis_at] // parts).reshape([-1 if axis == axis_at else 1 for axis in range(len(dims))])
    return level


def bell_draw(rng, dims, width, limit, cuts=(), held_as=jnp.bfloat16):
    gain = levels(rng, dims, cuts, -0.22, 0.18) if cuts else 1.0
    values = jax.random.normal(rng, dims, jnp.float32) * width * gain
    return jnp.minimum(jnp.maximum(values, -limit), limit).astype(held_as)


def setup_inputs(seed: int = 0) -> dict:
    keys = jax.random.split(jax.random.key(seed), 8)
    return {
        "env_in": bell_draw(keys[0], (MW, QA, QB, BB, KB), 1.0, 6.0, ((0, 8), (1, 4))),
        "ket_mps": bell_draw(keys[1], (PHYS, QA, QB, KB, KB), KB ** -0.5, 0.25, ((1, 4),)),
        "bra_mps": bell_draw(keys[2], (PHYS, QA, QB, BB, BB), BB ** -0.5, 0.375, ((1, 4),)),
        "ket_sizes": draw_ket_sizes(jax.random.fold_in(keys[7], 71), 0),
        "bra_sizes": draw_bra_sizes(jax.random.fold_in(keys[7], 71), 0),
        "entries": draw_entries(jax.random.fold_in(keys[7], 71), 0),
        "coeffs": bell_draw(keys[6], (MW, EPW), 1.0, 3.0, ((0, 8),), jnp.float32),
    }


def channel_charge(channel):
    klass = channel % 9
    return klass % 3 - 1, klass // 3 - 1


def keep_block(block, rows, cols):
    keep_rows = lax.broadcasted_iota(jnp.int32, block.shape, block.ndim - 2) < rows[..., None, None]
    keep_cols = lax.broadcasted_iota(jnp.int32, block.shape, block.ndim - 1) < cols[..., None, None]
    return jnp.where(keep_rows & keep_cols, block, jnp.zeros_like(block))


def reference(env_in, ket_mps, bra_mps, ket_sizes, bra_sizes, entries, coeffs):
    ket_ext = jnp.pad(ket_sizes, 2)
    bra_ext = jnp.pad(bra_sizes, 2)
    env_pad = jnp.pad(env_in, ((0, 0), (1, 0), (1, 0), (0, 0), (0, 0)))
    ket_pad = jnp.pad(ket_mps, ((0, 0), (1, 0), (1, 0), (0, 0), (0, 0)))
    bra_pad = jnp.pad(bra_mps, ((0, 0), (1, 1), (1, 1), (0, 0), (0, 0)))
    zero = jnp.zeros((), jnp.int32)

    def sizes_at(ext, shift_a, shift_b):
        return lax.dynamic_slice(ext, ((shift_a + 2).astype(jnp.int32), (shift_b + 2).astype(jnp.int32)), (QA, QB))

    def entry_term(item):
        chan = item // EPW
        slot = item % EPW
        out_w = entries[chan, slot, 0]
        phys_bra = entries[chan, slot, 1]
        phys_ket = entries[chan, slot, 2]
        value = coeffs[chan, slot]
        up_a = phys_ket % 2
        up_b = phys_ket // 2
        in_a, in_b = channel_charge(chan)
        out_a, out_b = channel_charge(out_w)
        env_blk = lax.dynamic_slice(env_pad, (chan.astype(jnp.int32), 1 - up_a, 1 - up_b, zero, zero), (1, QA, QB, BB, KB))[0]
        ket_blk = lax.dynamic_slice(ket_pad, (phys_ket, 1 - up_a, 1 - up_b, zero, zero), (1, QA, QB, KB, KB))[0]
        bra_blk = lax.dynamic_slice(bra_pad, (phys_bra, 1 + out_a, 1 + out_b, zero, zero), (1, QA, QB, BB, BB))[0]
        ket_src = sizes_at(ket_ext, -up_a, -up_b)
        env_blk = keep_block(env_blk, sizes_at(bra_ext, in_a - up_a, in_b - up_b), ket_src)
        ket_blk = keep_block(ket_blk, ket_src, sizes_at(ket_ext, zero, zero))
        bra_blk = keep_block(bra_blk, sizes_at(bra_ext, out_a - phys_bra % 2, out_b - phys_bra // 2), sizes_at(bra_ext, out_a, out_b))
        half = jnp.einsum("abik,abkl->abil", env_blk.astype(jnp.float32), ket_blk.astype(jnp.float32)).astype(jnp.bfloat16)
        term = jnp.einsum("abij,abil->abjl", bra_blk.astype(jnp.float32), half.astype(jnp.float32))
        return out_w, value * term

    def group(index, total):
        def step(inner, partial_value):
            item = (index * CH * EPW + inner).astype(jnp.int32)
            out_w, term = entry_term(item)
            return partial_value.at[out_w].add(term)

        partial_value = lax.fori_loop(0, CH * EPW, step, jnp.zeros((MW, QA, QB, BB, KB), jnp.float32))
        rounded = lax.optimization_barrier(partial_value.astype(jnp.bfloat16))
        return total + rounded.astype(jnp.float32)

    total = lax.fori_loop(0, N_ROW, group, jnp.zeros((MW, QA, QB, BB, KB), jnp.float32))
    return total.astype(jnp.bfloat16)
```

```python
import functools

import jax
import jax.numpy as jnp
from jax import lax
from jax.experimental import pallas as pl
from jax.experimental.pallas import tpu as pltpu
from jax.sharding import PartitionSpec as P

EPW = 8
Z = 4
DEPTH = 8
MESH = pl.DeviceIdType.MESH


def channel_charge(channel):
    klass = lax.rem(channel, 9)
    return lax.rem(klass, 3) - 1, lax.div(klass, 3) - 1


def ring_pos(row, n):
    wide = n // Z
    z, x = lax.div(row, wide), lax.rem(row, wide)
    t = jnp.where(lax.rem(z, 2) == 0, x - 1, wide - 1 - x)
    return jnp.where(x == 0, Z * (wide - 1) + Z - 1 - z, z * (wide - 1) + t)


def ring_row(pos, n):
    wide = n // Z
    z, t = lax.div(pos, wide - 1), lax.rem(pos, wide - 1)
    x = jnp.where(lax.rem(z, 2) == 0, 1 + t, wide - 1 - t)
    back = Z - 1 - (pos - Z * (wide - 1))
    return jnp.where(pos < Z * (wide - 1), z * wide + x, back * wide)


def gather_kernel(n, chans, sec_a, sec_b, env, bra, info, env_all, bra_all, info_all,
                  send, recv, isend, irecv, bsend, brecv, local):
    a = lax.axis_index("sec")
    row = lax.axis_index("row")
    pos = ring_pos(row, n)
    half = n // 2
    right, left = (ring_row(lax.rem(pos + d, n), n) for d in (1, n - 1))
    blocks = chans * sec_b

    barrier = pltpu.get_barrier_semaphore()
    for other in (right, left):
        pl.semaphore_signal(barrier, inc=1, device_id={"row": other}, device_id_type=MESH)
    for d in (-2, -1, 1, 2):
        @pl.when((a + d >= 0) & (a + d < sec_a))
        def _(d=d):
            pl.semaphore_signal(barrier, inc=1, device_id={"sec": a + d}, device_id_type=MESH)
    count = 2 + jnp.minimum(a, 2) + jnp.minimum(sec_a - 1 - a, 2)
    pl.semaphore_wait(barrier, count)

    def live(source, b):
        c_a, c_b = channel_charge(source * chans + b // sec_b)
        x, y = a + c_a, b % sec_b + c_b
        return (x >= 0) & (x < sec_a) & (y >= 0) & (y < sec_b)

    def source_at(k, way):
        return ring_row(lax.rem(pos + (n - k if way == 0 else k), n), n)

    def block_copy(k, way, b, source):
        src = env.at[b] if k == 1 else env_all.at[source * blocks + b]
        return pltpu.make_async_remote_copy(
            src_ref=src, dst_ref=env_all.at[source * blocks + b],
            send_sem=send.at[k - 1, way, b], recv_sem=recv.at[k - 1, way, b],
            device_id={"row": left if way else right}, device_id_type=MESH)

    def info_copy(k, way, source):
        src = info if k == 1 else info_all.at[source]
        return pltpu.make_async_remote_copy(
            src_ref=src, dst_ref=info_all.at[source],
            send_sem=isend.at[k - 1, way], recv_sem=irecv.at[k - 1, way],
            device_id={"row": left if way else right}, device_id_type=MESH)

    def used(k, way, b):
        return k < half or (b < blocks // 2) == (way == 0)

    def info_used(k, way):
        return k < half or way == 0

    def bra_copies():
        made = []
        for j, (d, slot) in enumerate(((1, 0), (-1, 2), (-2, 3))):
            made.append((d, pltpu.make_async_remote_copy(
                src_ref=bra, dst_ref=bra_all.at[slot],
                send_sem=bsend.at[j], recv_sem=brecv.at[j],
                device_id={"sec": a + d}, device_id_type=MESH)))
        return made

    for way in (0, 1):
        info_copy(1, way, row).start()
    for b in range(blocks):
        @pl.when(live(row, b))
        def _(b=b):
            for way in (0, 1):
                if used(1, way, b):
                    block_copy(1, way, b, row).start()
    for d, copy in bra_copies():
        @pl.when((a + d >= 0) & (a + d < sec_a))
        def _(copy=copy):
            copy.start()
    own = (
        pltpu.make_async_copy(env, env_all.at[pl.ds(row * blocks, blocks)], local.at[0]),
        pltpu.make_async_copy(bra, bra_all.at[1], local.at[1]),
        pltpu.make_async_copy(info, info_all.at[row], local.at[2]),
    )
    for copy in own:
        copy.start()

    for k in range(1, half + 1):
        sources = [source_at(k, way) for way in (0, 1)]
        for way in (0, 1):
            if info_used(k, way):
                info_copy(k, way, sources[way]).wait_recv()
                if k < half and info_used(k + 1, way):
                    info_copy(k + 1, way, sources[way]).start()
        for b in range(blocks):
            for way in (0, 1):
                if used(k, way, b):
                    @pl.when(live(sources[way], b))
                    def _(k=k, way=way, b=b):
                        block_copy(k, way, b, sources[way]).wait_recv()
                        if k < half and used(k + 1, way, b):
                            block_copy(k + 1, way, b, sources[way]).start()

    for k in range(1, half + 1):
        for way in (0, 1):
            source = row if k == 1 else source_at(k - 1, way)
            if info_used(k, way):
                info_copy(k, way, source).wait_send()
            for b in range(blocks):
                if used(k, way, b):
                    @pl.when(live(source, b))
                    def _(k=k, way=way, b=b, source=source):
                        block_copy(k, way, b, source).wait_send()
    for d, copy in bra_copies():
        @pl.when((a + d >= 0) & (a + d < sec_a))
        def _(copy=copy):
            copy.wait_send()

        @pl.when((a - d >= 0) & (a - d < sec_a))
        def _(copy=copy):
            copy.wait_recv()
    for copy in own:
        copy.wait()


def gather(env, bra, info, n, chans, sec_a, sec_b):
    half, blocks = n // 2, chans * sec_b
    anywhere = pl.BlockSpec(memory_space=pl.ANY)
    dma = pltpu.SemaphoreType.DMA
    return pl.pallas_call(
        functools.partial(gather_kernel, n, chans, sec_a, sec_b),
        out_shape=(
            jax.ShapeDtypeStruct((n * blocks,) + env.shape[1:], env.dtype),
            jax.ShapeDtypeStruct((4,) + bra.shape, bra.dtype),
            jax.ShapeDtypeStruct((n,) + info.shape, info.dtype),
        ),
        in_specs=[anywhere] * 3,
        out_specs=(anywhere,) * 3,
        scratch_shapes=[
            dma((half, 2, blocks)), dma((half, 2, blocks)), dma((half, 2)), dma((half, 2)),
            dma((3,)), dma((3,)), dma((3,)),
        ],
        compiler_params=pltpu.CompilerParams(collective_id=0, has_side_effects=True),
        name="gather_row",
    )(env, bra, info)


def terms_kernel(up_a, chans, starts, packed, values, ksz, env, bra, ket, out, buf, t_acc, acc, sems):
    first = starts[up_a * chans * 3]
    last = starts[(up_a + 1) * chans * 3]

    def fetch(j):
        slot = lax.rem(j, DEPTH)
        return pltpu.make_async_copy(env.at[lax.div(packed[j], 32)], buf.at[slot], sems.at[slot])

    for d in range(DEPTH):
        @pl.when(first + d < last)
        def _(d=d):
            fetch(first + d).start()

    acc[...] = jnp.zeros_like(acc)
    cols = lax.broadcasted_iota(jnp.int32, t_acc.shape, 1)

    def channel(i, carry):
        for kind, (up_b, q_b) in enumerate(((0, 0), (0, 1), (1, 0))):
            bucket = (up_a * chans + i) * 3 + kind
            begin, end = starts[bucket], starts[bucket + 1]

            @pl.when(end > begin)
            def _():
                t_acc[...] = jnp.zeros_like(t_acc)

                def item(j, c):
                    fetch(j).wait()
                    b = bra[lax.rem(packed[j], 32)]
                    e = buf[lax.rem(j, DEPTH)]
                    t_acc[...] += values[j] * jnp.dot(b, e, preferred_element_type=jnp.float32)

                    @pl.when(j + DEPTH < last)
                    def _():
                        fetch(j + DEPTH).start()
                    return c

                lax.fori_loop(begin, end, item, 0)
                t = jnp.where(cols < ksz[q_b], t_acc[...], 0.0).astype(jnp.bfloat16)
                k = ket[(up_a + 2 * up_b) * 2 + q_b]
                acc[i * 2 + up_b + q_b] += jnp.dot(t, k, preferred_element_type=jnp.float32)
        for p_b in (0, 1):
            block = acc[i * 2 + p_b]
            out[i * 2 + p_b] = jnp.where(cols < ksz[2 + p_b], block, 0.0).astype(out.dtype)
        return carry

    lax.fori_loop(0, chans, channel, 0)


def terms(up_a, chans, starts, packed, values, ksz, env, bra, ket, dtype):
    rows, cols = env.shape[1:]
    blocks = chans * 2
    smem = pl.BlockSpec(memory_space=pltpu.SMEM)
    vmem = pl.BlockSpec(memory_space=pltpu.VMEM)
    return pl.pallas_call(
        functools.partial(terms_kernel, up_a, chans),
        out_shape=jax.ShapeDtypeStruct((blocks, rows, cols), dtype),
        in_specs=[smem] * 4 + [pl.BlockSpec(memory_space=pl.ANY), vmem, vmem],
        out_specs=vmem,
        scratch_shapes=[
            pltpu.VMEM((DEPTH, rows, cols), env.dtype),
            pltpu.VMEM((rows, cols), jnp.float32),
            pltpu.VMEM((blocks, rows, cols), jnp.float32),
            pltpu.SemaphoreType.DMA((DEPTH,)),
        ],
        compiler_params=pltpu.CompilerParams(vmem_limit_bytes=40 * 1024 * 1024),
        cost_estimate=pl.CostEstimate(flops=5 * 10**9, bytes_accessed=16 * 2**20, transcendentals=0),
        name="terms_up" if up_a else "terms_same",
    )(starts, packed, values, ksz, env, bra, ket)


def body(env_in, ket_mps, bra_mps, ket_sizes, bra_sizes, entries, coeffs):
    chans, _, sec_b, bra_w, ket_w = env_in.shape
    a = lax.axis_index("sec")
    row = lax.axis_index("row")
    sec_a, n = lax.axis_size("sec"), lax.axis_size("row")
    ket_ext = jnp.pad(ket_sizes, 1)
    bra_ext = jnp.pad(bra_sizes, 2)

    def sizes_at(ext, pad, shift_a, shift_b):
        return lax.dynamic_slice(ext, (a + shift_a + pad, jnp.int32(shift_b + pad)), (1, sec_b))[0]

    own = sizes_at(bra_ext, 2, 0, 0)
    src = jnp.stack([sizes_at(bra_ext, 2, -(sp % 2), -(sp // 2)) for sp in range(4)])
    at = jnp.arange(bra_w, dtype=jnp.int32)
    keep = (at[None, None, :, None] < src[:, :, None, None]) & (at < own[None, :, None, None])
    bra = jnp.where(keep, bra_mps[:, 0], jnp.zeros((), bra_mps.dtype)).swapaxes(2, 3)
    bra = bra.reshape(4 * sec_b, bra_w, bra_w)

    code = (entries[..., 0] * 16 + entries[..., 1] * 4 + entries[..., 2]).astype(jnp.float32)
    mine = chans * EPW
    info = jnp.pad(jnp.stack([code.reshape(-1), coeffs.reshape(-1)]), ((0, 6), (0, 128 - mine)))

    env_all, bra_all, info_all = gather(
        env_in.reshape(chans * sec_b, bra_w, ket_w), bra, info, n, chans, sec_a, sec_b)
    bra_all = bra_all.reshape(4 * 4 * sec_b, bra_w, bra_w)

    code = info_all[:, 0, :mine].reshape(-1).astype(jnp.int32)
    value = info_all[:, 1, :mine].reshape(-1)
    wide = code.shape[0]
    code, value = jnp.tile(code, 2), jnp.tile(value, 2)
    index = jnp.arange(2 * wide, dtype=jnp.int32)
    q_b = index // wide
    w_in = (index % wide) // EPW
    w_out, sp, s = code // 16, (code // 4) % 4, code % 4
    up_a, up_b = s % 2, s // 2
    in_a, in_b = channel_charge(w_in)
    out_a, out_b = channel_charge(w_out)
    i = w_out - row * chans
    to_a, to_b = a + up_a + out_a, q_b + up_b + out_b

    def inside(x, count):
        return (x >= 0) & (x < count)

    live = (inside(i, chans) & inside(q_b + up_b, sec_b) & inside(a + up_a, sec_a)
            & inside(q_b + in_b, sec_b) & inside(a + in_a, sec_a)
            & inside(to_a, sec_a) & inside(to_b, sec_b))
    buckets = 2 * chans * 3
    key = jnp.where(live, (up_a * chans + i) * 3 + jnp.where(up_b == 0, q_b, 2), buckets)
    pack = (w_in * 2 + q_b) * 32 + (up_a + out_a + 1) * 8 + sp * 2 + to_b
    starts = jnp.sum(key[None, :] < jnp.arange(buckets + 1, dtype=jnp.int32)[:, None], axis=1, dtype=jnp.int32)
    order = key * (2 * wide) + index
    rank = jnp.sum(order[None, :] < order[:, None], axis=1, dtype=jnp.int32)
    hit = rank[None, :] == index[:, None]
    packed = jnp.sum(jnp.where(hit, pack[None, :], 0), axis=1, dtype=jnp.int32)
    values = jnp.sum(jnp.where(hit, value[None, :], 0.0), axis=1)

    ket = ket_mps.reshape(4 * sec_b, ket_w, ket_w)
    here = sizes_at(ket_ext, 1, 0, 0)
    above = sizes_at(ket_ext, 1, 1, 0)
    up = terms(1, chans, starts, packed, values, jnp.concatenate([here, above]), env_all, bra_all, ket, jnp.bfloat16)
    up = lax.ppermute(up, "sec", [(k, k + 1) for k in range(sec_a - 1)])
    same = terms(0, chans, starts, packed, values, jnp.concatenate([here, here]), env_all, bra_all, ket, jnp.float32)
    out = (same + up.astype(jnp.float32)).astype(env_in.dtype)
    return out.reshape(env_in.shape)


def solution(mesh):
    placed = (
        P("row", "sec", None, None, None),
        P(None, "sec", None, None, None),
        P(None, "sec", None, None, None),
        P(),
        P(),
        P("row", None, None),
        P("row", None),
    )
    return jax.shard_map(
        body,
        mesh=mesh,
        in_specs=placed,
        out_specs=P("row", "sec", None, None, None),
        check_vma=False,
    )
```

```python
import functools

import jax
import jax.numpy as jnp
from jax import lax
from jax.experimental import pallas as pl
from jax.experimental.pallas import tpu as pltpu
from jax.sharding import PartitionSpec as P

EPW = 8
Z = 4
DEPTH = 8
MESH = pl.DeviceIdType.MESH


def channel_charge(channel):
    klass = lax.rem(channel, 9)
    return lax.rem(klass, 3) - 1, lax.div(klass, 3) - 1


def ring_pos(row, n):
    wide = n // Z
    z, x = lax.div(row, wide), lax.rem(row, wide)
    t = jnp.where(lax.rem(z, 2) == 0, x - 1, wide - 1 - x)
    return jnp.where(x == 0, Z * (wide - 1) + Z - 1 - z, z * (wide - 1) + t)


def ring_row(pos, n):
    wide = n // Z
    z, t = lax.div(pos, wide - 1), lax.rem(pos, wide - 1)
    x = jnp.where(lax.rem(z, 2) == 0, 1 + t, wide - 1 - t)
    back = Z - 1 - (pos - Z * (wide - 1))
    return jnp.where(pos < Z * (wide - 1), z * wide + x, back * wide)


@functools.lru_cache(maxsize=None)
def hop_masks(n, chans, sec_b):
    wide, half, blocks = n // Z, n // 2, chans * sec_b
    order = [z * wide + (1 + t if z % 2 == 0 else wide - 1 - t) for z in range(Z) for t in range(wide - 1)]
    order += [z * wide for z in reversed(range(Z))]
    classes = []
    for dead in (-1, None, 1):
        items = []
        for p, source in enumerate(order):
            for b in range(blocks):
                klass = (source * chans + b // sec_b) % 9
                to_b = klass // 3 - 1 + b % sec_b
                if 0 <= to_b < sec_b and klass % 3 - 1 != dead:
                    items.append((p, source, b))
        reach = {item: half - (item[2] * 2 >= blocks) for item in items}

        def links(item, d):
            p = item[0]
            return [(0, (p + t) % n) for t in range(d)] + [(1, (p - 1 - t) % n) for t in range(n - 1 - d)]

        load = {(way, j): 0 for way in (0, 1) for j in range(n)}
        for item in items:
            for link in links(item, reach[item]):
                load[link] += 1
        for _ in range(12):
            for item in items:
                for link in links(item, reach[item]):
                    load[link] -= 1
                costs = []
                for d in range(half - 3, half + 3):
                    extra = sum((load[link] + 1) ** 6 - load[link] ** 6 for link in links(item, d))
                    costs.append((extra, abs(2 * d - n + 1), d))
                reach[item] = min(costs)[2]
                for link in links(item, reach[item]):
                    load[link] += 1
        classes.append((reach, max(load.values())))
    hops = max(max(d, n - 1 - d) for reach, _ in classes for d in reach.values())
    masks = [[[[0, 0, 0] for _ in range(blocks)] for _ in (0, 1)] for _ in range(hops)]
    for c, (reach, _) in enumerate(classes):
        for (p, source, b), d in reach.items():
            for way, count in ((0, d), (1, n - 1 - d)):
                for k in range(count):
                    masks[k][way][b][c] |= 1 << source
    return hops, masks, [top for _, top in classes]


def gather_kernel(n, chans, sec_a, sec_b, env, bra, info, env_all, bra_all, info_all,
                  send, recv, isend, irecv, bsend, brecv, local):
    a = lax.axis_index("sec")
    row = lax.axis_index("row")
    pos = ring_pos(row, n)
    half = n // 2
    right, left = (ring_row(lax.rem(pos + d, n), n) for d in (1, n - 1))
    blocks = chans * sec_b

    barrier = pltpu.get_barrier_semaphore()
    for other in (right, left):
        pl.semaphore_signal(barrier, inc=1, device_id={"row": other}, device_id_type=MESH)
    for d in (-2, -1, 1, 2):
        @pl.when((a + d >= 0) & (a + d < sec_a))
        def _(d=d):
            pl.semaphore_signal(barrier, inc=1, device_id={"sec": a + d}, device_id_type=MESH)
    count = 2 + jnp.minimum(a, 2) + jnp.minimum(sec_a - 1 - a, 2)
    pl.semaphore_wait(barrier, count)

    hops, masks, _ = hop_masks(n, chans, sec_b)

    def used(k, way, b):
        return k <= hops and any(masks[k - 1][way][b])

    def carried(k, way, b, source):
        low, inner, high = masks[k - 1][way][b]
        mask = jnp.where(a == 0, low, jnp.where(a == sec_a - 1, high, inner))
        return lax.rem(lax.shift_right_logical(mask, source), 2) == 1

    def source_at(k, way):
        return ring_row(lax.rem(pos + (n - k if way == 0 else k), n), n)

    def block_copy(k, way, b, source):
        src = env.at[b] if k == 1 else env_all.at[source * blocks + b]
        return pltpu.make_async_remote_copy(
            src_ref=src, dst_ref=env_all.at[source * blocks + b],
            send_sem=send.at[k - 1, way, b], recv_sem=recv.at[k - 1, way, b],
            device_id={"row": left if way else right}, device_id_type=MESH)

    def info_copy(k, way, source):
        src = info if k == 1 else info_all.at[source]
        return pltpu.make_async_remote_copy(
            src_ref=src, dst_ref=info_all.at[source],
            send_sem=isend.at[k - 1, way], recv_sem=irecv.at[k - 1, way],
            device_id={"row": left if way else right}, device_id_type=MESH)

    def info_used(k, way):
        return k < half or way == 0

    def bra_copies():
        made = []
        for j, (d, slot) in enumerate(((1, 0), (-1, 2), (-2, 3))):
            made.append((d, pltpu.make_async_remote_copy(
                src_ref=bra, dst_ref=bra_all.at[slot],
                send_sem=bsend.at[j], recv_sem=brecv.at[j],
                device_id={"sec": a + d}, device_id_type=MESH)))
        return made

    for way in (0, 1):
        info_copy(1, way, row).start()
    for b in range(blocks):
        for way in (0, 1):
            if used(1, way, b):
                @pl.when(carried(1, way, b, row))
                def _(b=b, way=way):
                    block_copy(1, way, b, row).start()
    for d, copy in bra_copies():
        @pl.when((a + d >= 0) & (a + d < sec_a))
        def _(copy=copy):
            copy.start()
    own = (
        pltpu.make_async_copy(env, env_all.at[pl.ds(row * blocks, blocks)], local.at[0]),
        pltpu.make_async_copy(bra, bra_all.at[1], local.at[1]),
        pltpu.make_async_copy(info, info_all.at[row], local.at[2]),
    )
    for copy in own:
        copy.start()

    for k in range(1, hops + 1):
        sources = [source_at(k, way) for way in (0, 1)]
        for way in (0, 1):
            if k <= half and info_used(k, way):
                info_copy(k, way, sources[way]).wait_recv()
                if k < half and info_used(k + 1, way):
                    info_copy(k + 1, way, sources[way]).start()
        for b in range(blocks):
            for way in (0, 1):
                if used(k, way, b):
                    @pl.when(carried(k, way, b, sources[way]))
                    def _(k=k, way=way, b=b):
                        block_copy(k, way, b, sources[way]).wait_recv()
                        if used(k + 1, way, b):
                            @pl.when(carried(k + 1, way, b, sources[way]))
                            def _():
                                block_copy(k + 1, way, b, sources[way]).start()

    for k in range(1, hops + 1):
        for way in (0, 1):
            source = row if k == 1 else source_at(k - 1, way)
            if k <= half and info_used(k, way):
                info_copy(k, way, source).wait_send()
            for b in range(blocks):
                if used(k, way, b):
                    @pl.when(carried(k, way, b, source))
                    def _(k=k, way=way, b=b, source=source):
                        block_copy(k, way, b, source).wait_send()
    for d, copy in bra_copies():
        @pl.when((a + d >= 0) & (a + d < sec_a))
        def _(copy=copy):
            copy.wait_send()

        @pl.when((a - d >= 0) & (a - d < sec_a))
        def _(copy=copy):
            copy.wait_recv()
    for copy in own:
        copy.wait()


def gather(env, bra, info, n, chans, sec_a, sec_b):
    half, blocks = n // 2, chans * sec_b
    hops = hop_masks(n, chans, sec_b)[0]
    anywhere = pl.BlockSpec(memory_space=pl.ANY)
    dma = pltpu.SemaphoreType.DMA
    return pl.pallas_call(
        functools.partial(gather_kernel, n, chans, sec_a, sec_b),
        out_shape=(
            jax.ShapeDtypeStruct((n * blocks,) + env.shape[1:], env.dtype),
            jax.ShapeDtypeStruct((4,) + bra.shape, bra.dtype),
            jax.ShapeDtypeStruct((n,) + info.shape, info.dtype),
        ),
        in_specs=[anywhere] * 3,
        out_specs=(anywhere,) * 3,
        scratch_shapes=[
            dma((hops, 2, blocks)), dma((hops, 2, blocks)), dma((half, 2)), dma((half, 2)),
            dma((3,)), dma((3,)), dma((3,)),
        ],
        compiler_params=pltpu.CompilerParams(collective_id=0, has_side_effects=True),
        name="gather_row",
    )(env, bra, info)


def terms_kernel(up_a, base, count, starts, packed, values, ksz, env, bra_hbm, ket_hbm, out,
                 buf, bra, ket, t_acc, acc, sems, load):
    first = starts[base * 3]
    last = starts[(base + count) * 3]
    loads = [pltpu.make_async_copy(bra_hbm.at[pl.ds(8 * up_a, 24)], bra, load.at[0])]
    loads += [
        pltpu.make_async_copy(ket_hbm.at[(up_a + 2 * (j // 2)) * 2 + j % 2], ket.at[j], load.at[1 + j])
        for j in range(3)
    ]
    loads[0].start()

    def fetch(j):
        slot = lax.rem(j, DEPTH)
        return pltpu.make_async_copy(env.at[lax.div(packed[j], 32)], buf.at[slot], sems.at[slot])

    for d in range(DEPTH):
        @pl.when(first + d < last)
        def _(d=d):
            fetch(first + d).start()

    for copy in loads[1:]:
        copy.start()
    acc[...] = jnp.zeros_like(acc)
    cols = lax.broadcasted_iota(jnp.int32, t_acc.shape, 1)

    for copy in loads:
        copy.wait()

    def channel(i, carry):
        for kind, (up_b, q_b) in enumerate(((0, 0), (0, 1), (1, 0))):
            bucket = (base + i) * 3 + kind
            begin, end = starts[bucket], starts[bucket + 1]

            @pl.when(end > begin)
            def _():
                t_acc[...] = jnp.zeros_like(t_acc)

                def item(j, c):
                    fetch(j).wait()
                    b = bra[lax.rem(packed[j], 32) - 8 * up_a]
                    e = buf[lax.rem(j, DEPTH)]
                    t_acc[...] += values[j] * jnp.dot(b, e, preferred_element_type=jnp.float32)

                    @pl.when(j + DEPTH < last)
                    def _():
                        fetch(j + DEPTH).start()
                    return c

                lax.fori_loop(begin, end, item, 0)
                t = jnp.where(cols < ksz[q_b], t_acc[...], 0.0).astype(jnp.bfloat16)
                k = ket[2 * up_b + q_b]
                acc[i * 2 + up_b + q_b] += jnp.dot(t, k, preferred_element_type=jnp.float32)
        for p_b in (0, 1):
            block = acc[i * 2 + p_b]
            out[i * 2 + p_b] = jnp.where(cols < ksz[2 + p_b], block, 0.0).astype(out.dtype)
        return carry

    lax.fori_loop(0, count, channel, 0)


def terms(up_a, chans, at, count, starts, packed, values, ksz, env, bra, ket, dtype):
    rows, cols = env.shape[1:]
    blocks = count * 2
    smem = pl.BlockSpec(memory_space=pltpu.SMEM)
    return pl.pallas_call(
        functools.partial(terms_kernel, up_a, up_a * chans + at, count),
        out_shape=jax.ShapeDtypeStruct((blocks, rows, cols), dtype),
        in_specs=[smem] * 4 + [pl.BlockSpec(memory_space=pl.ANY)] * 3,
        out_specs=pl.BlockSpec(memory_space=pltpu.VMEM),
        scratch_shapes=[
            pltpu.VMEM((DEPTH, rows, cols), env.dtype),
            pltpu.VMEM((24,) + bra.shape[1:], bra.dtype),
            pltpu.VMEM((3,) + ket.shape[1:], ket.dtype),
            pltpu.VMEM((rows, cols), jnp.float32),
            pltpu.VMEM((blocks, rows, cols), jnp.float32),
            pltpu.SemaphoreType.DMA((DEPTH,)),
            pltpu.SemaphoreType.DMA((4,)),
        ],
        compiler_params=pltpu.CompilerParams(vmem_limit_bytes=40 * 1024 * 1024),
        cost_estimate=pl.CostEstimate(flops=5 * 10**9, bytes_accessed=16 * 2**20, transcendentals=0),
        name="terms_up" if up_a else "terms_same",
    )(starts, packed, values, ksz, env, bra, ket)


def body(env_in, ket_mps, bra_mps, ket_sizes, bra_sizes, entries, coeffs):
    chans, _, sec_b, bra_w, ket_w = env_in.shape
    a = lax.axis_index("sec")
    row = lax.axis_index("row")
    sec_a, n = lax.axis_size("sec"), lax.axis_size("row")
    ket_ext = jnp.pad(ket_sizes, 1)
    bra_ext = jnp.pad(bra_sizes, 2)

    def sizes_at(ext, pad, shift_a, shift_b):
        return lax.dynamic_slice(ext, (a + shift_a + pad, jnp.int32(shift_b + pad)), (1, sec_b))[0]

    own = sizes_at(bra_ext, 2, 0, 0)
    src = jnp.stack([sizes_at(bra_ext, 2, -(sp % 2), -(sp // 2)) for sp in range(4)])
    at = jnp.arange(bra_w, dtype=jnp.int32)
    keep = (at[None, None, :, None] < src[:, :, None, None]) & (at < own[None, :, None, None])
    bra = jnp.where(keep, bra_mps[:, 0], jnp.zeros((), bra_mps.dtype)).swapaxes(2, 3)
    bra = bra.reshape(4 * sec_b, bra_w, bra_w)

    code = (entries[..., 0] * 16 + entries[..., 1] * 4 + entries[..., 2]).astype(jnp.float32)
    mine = chans * EPW
    info = jnp.pad(jnp.stack([code.reshape(-1), coeffs.reshape(-1)]), ((0, 6), (0, 128 - mine)))

    env_all, bra_all, info_all = gather(
        env_in.reshape(chans * sec_b, bra_w, ket_w), bra, info, n, chans, sec_a, sec_b)
    bra_all = bra_all.reshape(4 * 4 * sec_b, bra_w, bra_w)

    code = info_all[:, 0, :mine].reshape(-1).astype(jnp.int32)
    value = info_all[:, 1, :mine].reshape(-1)
    wide = code.shape[0]
    code, value = jnp.tile(code, 2), jnp.tile(value, 2)
    index = jnp.arange(2 * wide, dtype=jnp.int32)
    q_b = index // wide
    w_in = (index % wide) // EPW
    w_out, sp, s = code // 16, (code // 4) % 4, code % 4
    up_a, up_b = s % 2, s // 2
    in_a, in_b = channel_charge(w_in)
    out_a, out_b = channel_charge(w_out)
    i = w_out - row * chans
    to_a, to_b = a + up_a + out_a, q_b + up_b + out_b

    def inside(x, count):
        return (x >= 0) & (x < count)

    live = (inside(i, chans) & inside(q_b + up_b, sec_b) & inside(a + up_a, sec_a)
            & inside(q_b + in_b, sec_b) & inside(a + in_a, sec_a)
            & inside(to_a, sec_a) & inside(to_b, sec_b))
    buckets = 2 * chans * 3
    key = jnp.where(live, (up_a * chans + i) * 3 + jnp.where(up_b == 0, q_b, 2), buckets)
    pack = (w_in * 2 + q_b) * 32 + (up_a + out_a + 1) * 8 + sp * 2 + to_b
    starts = jnp.sum(key[None, :] < jnp.arange(buckets + 1, dtype=jnp.int32)[:, None], axis=1, dtype=jnp.int32)
    order = key * (2 * wide) + index
    rank = jnp.sum(order[None, :] < order[:, None], axis=1, dtype=jnp.int32)
    hit = rank[None, :] == index[:, None]
    packed = jnp.sum(jnp.where(hit, pack[None, :], 0), axis=1, dtype=jnp.int32)
    values = jnp.sum(jnp.where(hit, value[None, :], 0.0), axis=1)

    ket = ket_mps.reshape(4 * sec_b, ket_w, ket_w)
    here = sizes_at(ket_ext, 1, 0, 0)
    above = sizes_at(ket_ext, 1, 1, 0)
    sent = []
    part = chans // 2
    for at in (0, part):
        up = terms(1, chans, at, part, starts, packed, values, jnp.concatenate([here, above]),
                   env_all, bra_all, ket, jnp.bfloat16)
        sent.append(lax.ppermute(up, "sec", [(k, k + 1) for k in range(sec_a - 1)]))
    same = terms(0, chans, 0, chans, starts, packed, values, jnp.concatenate([here, here]),
                 env_all, bra_all, ket, jnp.float32)
    out = (same + jnp.concatenate(sent).astype(jnp.float32)).astype(env_in.dtype)
    return out.reshape(env_in.shape)


def solution(mesh):
    placed = (
        P("row", "sec", None, None, None),
        P(None, "sec", None, None, None),
        P(None, "sec", None, None, None),
        P(),
        P(),
        P("row", None, None),
        P("row", None),
    )
    return jax.shard_map(
        body,
        mesh=mesh,
        in_specs=placed,
        out_specs=P("row", "sec", None, None, None),
        check_vma=False,
    )
```

```python
import functools

import jax
import jax.numpy as jnp
from jax import lax
from jax.experimental import pallas as pl
from jax.experimental.pallas import tpu as pltpu
from jax.sharding import PartitionSpec as P

EPW = 8
Z = 4
DEPTH = 8
MESH = pl.DeviceIdType.MESH


def channel_charge(channel):
    klass = lax.rem(channel, 9)
    return lax.rem(klass, 3) - 1, lax.div(klass, 3) - 1


def ring_pos(row, n):
    wide = n // Z
    z, x = lax.div(row, wide), lax.rem(row, wide)
    t = jnp.where(lax.rem(z, 2) == 0, x - 1, wide - 1 - x)
    return jnp.where(x == 0, Z * (wide - 1) + Z - 1 - z, z * (wide - 1) + t)


def ring_row(pos, n):
    wide = n // Z
    z, t = lax.div(pos, wide - 1), lax.rem(pos, wide - 1)
    x = jnp.where(lax.rem(z, 2) == 0, 1 + t, wide - 1 - t)
    back = Z - 1 - (pos - Z * (wide - 1))
    return jnp.where(pos < Z * (wide - 1), z * wide + x, back * wide)


@functools.lru_cache(maxsize=None)
def hop_masks(n, chans, sec_b):
    wide, half, blocks = n // Z, n // 2, chans * sec_b
    order = [z * wide + (1 + t if z % 2 == 0 else wide - 1 - t) for z in range(Z) for t in range(wide - 1)]
    order += [z * wide for z in reversed(range(Z))]
    classes = []
    for dead in (-1, None, 1):
        items = []
        for p, source in enumerate(order):
            for b in range(blocks):
                klass = (source * chans + b // sec_b) % 9
                to_b = klass // 3 - 1 + b % sec_b
                if 0 <= to_b < sec_b and klass % 3 - 1 != dead:
                    items.append((p, source, b))
        reach = {item: half - (item[2] * 2 >= blocks) for item in items}

        def links(item, d):
            p = item[0]
            return [(0, (p + t) % n) for t in range(d)] + [(1, (p - 1 - t) % n) for t in range(n - 1 - d)]

        load = {(way, j): 0 for way in (0, 1) for j in range(n)}
        for item in items:
            for link in links(item, reach[item]):
                load[link] += 1
        for _ in range(12):
            for item in items:
                for link in links(item, reach[item]):
                    load[link] -= 1
                costs = []
                for d in range(half - 3, half + 3):
                    extra = sum((load[link] + 1) ** 6 - load[link] ** 6 for link in links(item, d))
                    costs.append((extra, abs(2 * d - n + 1), d))
                reach[item] = min(costs)[2]
                for link in links(item, reach[item]):
                    load[link] += 1
        classes.append((reach, max(load.values())))
    hops = max(max(d, n - 1 - d) for reach, _ in classes for d in reach.values())
    masks = [[[[0, 0, 0] for _ in range(blocks)] for _ in (0, 1)] for _ in range(hops)]
    for c, (reach, _) in enumerate(classes):
        for (p, source, b), d in reach.items():
            for way, count in ((0, d), (1, n - 1 - d)):
                for k in range(count):
                    masks[k][way][b][c] |= 1 << source
    return hops, masks, [top for _, top in classes]


def gather_kernel(n, chans, sec_a, sec_b, sizes, env, bra_hbm, info, env_all, bra_all, info_all,
                  env_own, bra_raw, bra, send, recv, isend, irecv, bsend, brecv, local):
    a = lax.axis_index("sec")
    row = lax.axis_index("row")
    pos = ring_pos(row, n)
    half = n // 2
    right, left = (ring_row(lax.rem(pos + d, n), n) for d in (1, n - 1))
    blocks = chans * sec_b

    barrier = pltpu.get_barrier_semaphore()
    for other in (right, left):
        pl.semaphore_signal(barrier, inc=1, device_id={"row": other}, device_id_type=MESH)
    for d in (-2, -1, 1, 2):
        @pl.when((a + d >= 0) & (a + d < sec_a))
        def _(d=d):
            pl.semaphore_signal(barrier, inc=1, device_id={"sec": a + d}, device_id_type=MESH)
    count = 2 + jnp.minimum(a, 2) + jnp.minimum(sec_a - 1 - a, 2)
    pl.semaphore_wait(barrier, count)

    hops, masks, _ = hop_masks(n, chans, sec_b)

    def used(k, way, b):
        return k <= hops and any(masks[k - 1][way][b])

    def carried(k, way, b, source):
        low, inner, high = masks[k - 1][way][b]
        mask = jnp.where(a == 0, low, jnp.where(a == sec_a - 1, high, inner))
        return lax.rem(lax.shift_right_logical(mask, source), 2) == 1

    def source_at(k, way):
        return ring_row(lax.rem(pos + (n - k if way == 0 else k), n), n)

    def block_copy(k, way, b, source):
        src = env.at[b] if k == 1 else env_all.at[source * blocks + b]
        return pltpu.make_async_remote_copy(
            src_ref=src, dst_ref=env_all.at[source * blocks + b],
            send_sem=send.at[k - 1, way, b], recv_sem=recv.at[k - 1, way, b],
            device_id={"row": left if way else right}, device_id_type=MESH)

    def info_copy(k, way, source):
        src = info if k == 1 else info_all.at[source]
        return pltpu.make_async_remote_copy(
            src_ref=src, dst_ref=info_all.at[source],
            send_sem=isend.at[k - 1, way], recv_sem=irecv.at[k - 1, way],
            device_id={"row": left if way else right}, device_id_type=MESH)

    def info_used(k, way):
        return k < half or way == 0

    def bra_copies():
        made = []
        for j, (d, slot) in enumerate(((1, 0), (-1, 2), (-2, 3))):
            made.append((d, pltpu.make_async_remote_copy(
                src_ref=bra, dst_ref=bra_all.at[slot],
                send_sem=bsend.at[j], recv_sem=brecv.at[j],
                device_id={"sec": a + d}, device_id_type=MESH)))
        return made

    for way in (0, 1):
        info_copy(1, way, row).start()
    for b in range(blocks):
        for way in (0, 1):
            if used(1, way, b):
                @pl.when(carried(1, way, b, row))
                def _(b=b, way=way):
                    block_copy(1, way, b, row).start()
    loads = (
        pltpu.make_async_copy(bra_hbm, bra_raw, local.at[0]),
        pltpu.make_async_copy(env, env_own, local.at[1]),
    )
    for copy in loads:
        copy.start()
    info_own = pltpu.make_async_copy(info, info_all.at[row], local.at[2])
    info_own.start()

    def size_at(x, y):
        inner = jnp.where((x >= 0) & (y >= 0), sizes[jnp.maximum(x, 0) * sec_b + max(y, 0)], 0)
        return inner

    loads[0].wait()
    at_row = lax.broadcasted_iota(jnp.int32, bra.shape[1:], 0)
    at_col = lax.broadcasted_iota(jnp.int32, bra.shape[1:], 1)
    for j in range(4 * sec_b):
        sp, y = j // sec_b, j % sec_b
        keep = (at_row < size_at(a - sp % 2, y - sp // 2)) & (at_col < size_at(a, y))
        block = jnp.where(keep, bra_raw[j].astype(jnp.float32), 0.0)
        bra[j] = block.T.astype(bra.dtype)
    for d, copy in bra_copies():
        @pl.when((a + d >= 0) & (a + d < sec_a))
        def _(copy=copy):
            copy.start()
    loads[1].wait()
    own = (
        pltpu.make_async_copy(env_own, env_all.at[pl.ds(row * blocks, blocks)], local.at[1]),
        pltpu.make_async_copy(bra, bra_all.at[1], local.at[0]),
        info_own,
    )
    for copy in own[:2]:
        copy.start()

    for k in range(1, hops + 1):
        sources = [source_at(k, way) for way in (0, 1)]
        for way in (0, 1):
            if k <= half and info_used(k, way):
                info_copy(k, way, sources[way]).wait_recv()
                if k < half and info_used(k + 1, way):
                    info_copy(k + 1, way, sources[way]).start()
        for b in range(blocks):
            for way in (0, 1):
                if used(k, way, b):
                    @pl.when(carried(k, way, b, sources[way]))
                    def _(k=k, way=way, b=b):
                        block_copy(k, way, b, sources[way]).wait_recv()
                        if used(k + 1, way, b):
                            @pl.when(carried(k + 1, way, b, sources[way]))
                            def _():
                                block_copy(k + 1, way, b, sources[way]).start()

    for k in range(1, hops + 1):
        for way in (0, 1):
            source = row if k == 1 else source_at(k - 1, way)
            if k <= half and info_used(k, way):
                info_copy(k, way, source).wait_send()
            for b in range(blocks):
                if used(k, way, b):
                    @pl.when(carried(k, way, b, source))
                    def _(k=k, way=way, b=b, source=source):
                        block_copy(k, way, b, source).wait_send()
    for d, copy in bra_copies():
        @pl.when((a + d >= 0) & (a + d < sec_a))
        def _(copy=copy):
            copy.wait_send()

        @pl.when((a - d >= 0) & (a - d < sec_a))
        def _(copy=copy):
            copy.wait_recv()
    for copy in own:
        copy.wait()


def gather(sizes, env, bra, info, n, chans, sec_a, sec_b):
    half, blocks = n // 2, chans * sec_b
    hops = hop_masks(n, chans, sec_b)[0]
    anywhere = pl.BlockSpec(memory_space=pl.ANY)
    dma = pltpu.SemaphoreType.DMA
    return pl.pallas_call(
        functools.partial(gather_kernel, n, chans, sec_a, sec_b),
        out_shape=(
            jax.ShapeDtypeStruct((n * blocks,) + env.shape[1:], env.dtype),
            jax.ShapeDtypeStruct((4,) + bra.shape, bra.dtype),
            jax.ShapeDtypeStruct((n,) + info.shape, info.dtype),
        ),
        in_specs=[pl.BlockSpec(memory_space=pltpu.SMEM)] + [anywhere] * 3,
        out_specs=(anywhere,) * 3,
        scratch_shapes=[
            pltpu.VMEM(env.shape, env.dtype), pltpu.VMEM(bra.shape, bra.dtype), pltpu.VMEM(bra.shape, bra.dtype),
            dma((hops, 2, blocks)), dma((hops, 2, blocks)), dma((half, 2)), dma((half, 2)),
            dma((3,)), dma((3,)), dma((3,)),
        ],
        compiler_params=pltpu.CompilerParams(
            collective_id=0, has_side_effects=True, vmem_limit_bytes=60 * 1024 * 1024),
        name="gather_row",
    )(sizes, env, bra, info)


def terms_kernel(up_a, base, count, starts, packed, values, ksz, env, bra_hbm, ket_hbm, out,
                 buf, bra, ket, t_acc, acc, sems, load):
    first = starts[base * 3]
    last = starts[(base + count) * 3]
    loads = [pltpu.make_async_copy(bra_hbm.at[pl.ds(8 * up_a, 24)], bra, load.at[0])]
    loads += [
        pltpu.make_async_copy(ket_hbm.at[(up_a + 2 * (j // 2)) * 2 + j % 2], ket.at[j], load.at[1 + j])
        for j in range(3)
    ]
    loads[0].start()

    def fetch(j):
        slot = lax.rem(j, DEPTH)
        return pltpu.make_async_copy(env.at[lax.div(packed[j], 32)], buf.at[slot], sems.at[slot])

    for d in range(DEPTH):
        @pl.when(first + d < last)
        def _(d=d):
            fetch(first + d).start()

    for copy in loads[1:]:
        copy.start()
    acc[...] = jnp.zeros_like(acc)
    cols = lax.broadcasted_iota(jnp.int32, t_acc.shape, 1)

    for copy in loads:
        copy.wait()

    def channel(i, carry):
        for kind, (up_b, q_b) in enumerate(((0, 0), (0, 1), (1, 0))):
            bucket = (base + i) * 3 + kind
            begin, end = starts[bucket], starts[bucket + 1]

            @pl.when(end > begin)
            def _():
                t_acc[...] = jnp.zeros_like(t_acc)

                def item(j, c):
                    fetch(j).wait()
                    b = bra[lax.rem(packed[j], 32) - 8 * up_a]
                    e = buf[lax.rem(j, DEPTH)]
                    t_acc[...] += values[j] * jnp.dot(b, e, preferred_element_type=jnp.float32)

                    @pl.when(j + DEPTH < last)
                    def _():
                        fetch(j + DEPTH).start()
                    return c

                lax.fori_loop(begin, end, item, 0)
                t = jnp.where(cols < ksz[q_b], t_acc[...], 0.0).astype(jnp.bfloat16)
                k = ket[2 * up_b + q_b]
                acc[i * 2 + up_b + q_b] += jnp.dot(t, k, preferred_element_type=jnp.float32)
        for p_b in (0, 1):
            block = acc[i * 2 + p_b]
            out[i * 2 + p_b] = jnp.where(cols < ksz[2 + p_b], block, 0.0).astype(out.dtype)
        return carry

    lax.fori_loop(0, count, channel, 0)


def terms(up_a, chans, at, count, starts, packed, values, ksz, env, bra, ket, dtype):
    rows, cols = env.shape[1:]
    blocks = count * 2
    smem = pl.BlockSpec(memory_space=pltpu.SMEM)
    return pl.pallas_call(
        functools.partial(terms_kernel, up_a, up_a * chans + at, count),
        out_shape=jax.ShapeDtypeStruct((blocks, rows, cols), dtype),
        in_specs=[smem] * 4 + [pl.BlockSpec(memory_space=pl.ANY)] * 3,
        out_specs=pl.BlockSpec(memory_space=pltpu.VMEM),
        scratch_shapes=[
            pltpu.VMEM((DEPTH, rows, cols), env.dtype),
            pltpu.VMEM((24,) + bra.shape[1:], bra.dtype),
            pltpu.VMEM((3,) + ket.shape[1:], ket.dtype),
            pltpu.VMEM((rows, cols), jnp.float32),
            pltpu.VMEM((blocks, rows, cols), jnp.float32),
            pltpu.SemaphoreType.DMA((DEPTH,)),
            pltpu.SemaphoreType.DMA((4,)),
        ],
        compiler_params=pltpu.CompilerParams(vmem_limit_bytes=60 * 1024 * 1024),
        cost_estimate=pl.CostEstimate(flops=5 * 10**9, bytes_accessed=16 * 2**20, transcendentals=0),
        name="terms_up" if up_a else "terms_same",
    )(starts, packed, values, ksz, env, bra, ket)


def body(env_in, ket_mps, bra_mps, ket_sizes, bra_sizes, entries, coeffs):
    chans, _, sec_b, bra_w, ket_w = env_in.shape
    a = lax.axis_index("sec")
    row = lax.axis_index("row")
    sec_a, n = lax.axis_size("sec"), lax.axis_size("row")
    ket_ext = jnp.pad(ket_sizes, 1)

    def sizes_at(ext, pad, shift_a, shift_b):
        return lax.dynamic_slice(ext, (a + shift_a + pad, jnp.int32(shift_b + pad)), (1, sec_b))[0]

    bra = bra_mps.reshape(4 * sec_b, bra_w, bra_w)
    code = (entries[..., 0] * 16 + entries[..., 1] * 4 + entries[..., 2]).astype(jnp.float32)
    mine = chans * EPW
    info = jnp.pad(jnp.stack([code.reshape(-1), coeffs.reshape(-1)]), ((0, 6), (0, 128 - mine)))

    env_all, bra_all, info_all = gather(
        bra_sizes.reshape(-1), env_in.reshape(chans * sec_b, bra_w, ket_w), bra, info, n, chans, sec_a, sec_b)
    bra_all = bra_all.reshape(4 * 4 * sec_b, bra_w, bra_w)

    code = info_all[:, 0, :mine].reshape(-1).astype(jnp.int32)
    value = info_all[:, 1, :mine].reshape(-1)
    wide = code.shape[0]
    code, value = jnp.tile(code, 2), jnp.tile(value, 2)
    index = jnp.arange(2 * wide, dtype=jnp.int32)
    q_b = index // wide
    w_in = (index % wide) // EPW
    w_out, sp, s = code // 16, (code // 4) % 4, code % 4
    up_a, up_b = s % 2, s // 2
    in_a, in_b = channel_charge(w_in)
    out_a, out_b = channel_charge(w_out)
    i = w_out - row * chans
    to_a, to_b = a + up_a + out_a, q_b + up_b + out_b

    def inside(x, count):
        return (x >= 0) & (x < count)

    live = (inside(i, chans) & inside(q_b + up_b, sec_b) & inside(a + up_a, sec_a)
            & inside(q_b + in_b, sec_b) & inside(a + in_a, sec_a)
            & inside(to_a, sec_a) & inside(to_b, sec_b))
    buckets = 2 * chans * 3
    key = jnp.where(live, (up_a * chans + i) * 3 + jnp.where(up_b == 0, q_b, 2), buckets)
    pack = (w_in * 2 + q_b) * 32 + (up_a + out_a + 1) * 8 + sp * 2 + to_b
    starts = jnp.sum(key[None, :] < jnp.arange(buckets + 1, dtype=jnp.int32)[:, None], axis=1, dtype=jnp.int32)
    order = key * (2 * wide) + index
    rank = jnp.sum(order[None, :] < order[:, None], axis=1, dtype=jnp.int32)
    hit = rank[None, :] == index[:, None]
    packed = jnp.sum(jnp.where(hit, pack[None, :], 0), axis=1, dtype=jnp.int32)
    values = jnp.sum(jnp.where(hit, value[None, :], 0.0), axis=1)

    ket = ket_mps.reshape(4 * sec_b, ket_w, ket_w)
    here = sizes_at(ket_ext, 1, 0, 0)
    above = sizes_at(ket_ext, 1, 1, 0)
    sent = []
    part = chans // 2
    for at in (0, part):
        up = terms(1, chans, at, part, starts, packed, values, jnp.concatenate([here, above]),
                   env_all, bra_all, ket, jnp.bfloat16)
        sent.append(lax.ppermute(up, "sec", [(k, k + 1) for k in range(sec_a - 1)]))
    same = terms(0, chans, 0, chans, starts, packed, values, jnp.concatenate([here, here]),
                 env_all, bra_all, ket, jnp.float32)
    out = (same + jnp.concatenate(sent).astype(jnp.float32)).astype(env_in.dtype)
    return out.reshape(env_in.shape)


def solution(mesh):
    placed = (
        P("row", "sec", None, None, None),
        P(None, "sec", None, None, None),
        P(None, "sec", None, None, None),
        P(),
        P(),
        P("row", None, None),
        P("row", None),
    )
    return jax.shard_map(
        body,
        mesh=mesh,
        in_specs=placed,
        out_specs=P("row", "sec", None, None, None),
        check_vma=False,
    )
```

```python
import functools

import jax
import jax.numpy as jnp
from jax import lax
from jax.experimental import pallas as pl
from jax.experimental.pallas import tpu as pltpu
from jax.sharding import PartitionSpec as P

EPW = 8
Z = 4
DEPTH = 8
MESH = pl.DeviceIdType.MESH


def channel_charge(channel):
    klass = lax.rem(channel, 9)
    return lax.rem(klass, 3) - 1, lax.div(klass, 3) - 1


def ring_pos(row, n):
    wide = n // Z
    z, x = lax.div(row, wide), lax.rem(row, wide)
    t = jnp.where(lax.rem(z, 2) == 0, x - 1, wide - 1 - x)
    return jnp.where(x == 0, Z * (wide - 1) + Z - 1 - z, z * (wide - 1) + t)


def ring_row(pos, n):
    wide = n // Z
    z, t = lax.div(pos, wide - 1), lax.rem(pos, wide - 1)
    x = jnp.where(lax.rem(z, 2) == 0, 1 + t, wide - 1 - t)
    back = Z - 1 - (pos - Z * (wide - 1))
    return jnp.where(pos < Z * (wide - 1), z * wide + x, back * wide)


@functools.lru_cache(maxsize=None)
def hop_masks(n, chans, sec_b):
    wide, half, blocks = n // Z, n // 2, chans * sec_b
    order = [z * wide + (1 + t if z % 2 == 0 else wide - 1 - t) for z in range(Z) for t in range(wide - 1)]
    order += [z * wide for z in reversed(range(Z))]
    classes = {}
    shared = None
    for dead in (None, -1, 1):
        items = []
        for p, source in enumerate(order):
            for b in range(blocks):
                klass = (source * chans + b // sec_b) % 9
                to_b = klass // 3 - 1 + b % sec_b
                if 0 <= to_b < sec_b and klass % 3 - 1 != dead:
                    items.append((p, source, b))
        reach = {item: half - (item[2] * 2 >= blocks) for item in items}

        def links(item, d):
            p = item[0]
            return [(0, (p + t) % n) for t in range(d)] + [(1, (p - 1 - t) % n) for t in range(n - 1 - d)]

        load = dict(shared) if shared else {(way, j): 0 for way in (0, 1) for j in range(n)}
        for item in items:
            for link in links(item, reach[item]):
                load[link] += 1
        for _ in range(12):
            for item in items:
                for link in links(item, reach[item]):
                    load[link] -= 1
                costs = []
                for d in range(half - 2, half + 2):
                    extra = sum((load[link] + 1) ** 6 - load[link] ** 6 for link in links(item, d))
                    costs.append((extra, abs(2 * d - n + 1), d))
                reach[item] = min(costs)[2]
                for link in links(item, reach[item]):
                    load[link] += 1
        classes[dead] = (reach, max(load.values()))
        shared = shared or load
    classes = [classes[dead] for dead in (-1, None, 1)]
    hops = max(max(d, n - 1 - d) for reach, _ in classes for d in reach.values())
    masks = [[[[0, 0, 0] for _ in range(blocks)] for _ in (0, 1)] for _ in range(hops)]
    for c, (reach, _) in enumerate(classes):
        for (p, source, b), d in reach.items():
            for way, count in ((0, d), (1, n - 1 - d)):
                for k in range(count):
                    masks[k][way][b][c] |= 1 << source
    return hops, masks, [top for _, top in classes]


def fill_lists(n, chans, sec_a, sec_b, a, row, info, info_all, held, ints, floats, sem):
    for source in range(n):
        @pl.when(row == source)
        def _(source=source):
            copy = pltpu.make_async_copy(info, held.at[source], sem)
            copy.start()
            copy.wait()

        @pl.when(row != source)
        def _(source=source):
            copy = pltpu.make_async_copy(info_all.at[source], held.at[source], sem)
            copy.start()
            copy.wait()
    mine = chans * EPW
    wide = n * mine
    buckets = 2 * chans * 3

    def inside(x, count):
        return (x >= 0) & (x < count)

    def keys(code, index, q_b):
        def field(at, bits=2):
            return lax.shift_right_logical(code, at) & ((1 << bits) - 1)

        out_b, out_a, in_b, in_a = (field(2 * j) - 1 for j in range(4))
        s, sp, w_in, w_out = field(8), field(10), field(12, 5), field(17, 5)
        up_a, up_b = s & 1, lax.shift_right_logical(s, 1)
        i = w_out - row * chans
        to_b = up_b + out_b + q_b
        live = (inside(i, chans) & inside(up_b + q_b, sec_b) & inside(up_a + a, sec_a)
                & inside(in_b + q_b, sec_b) & inside(in_a + a, sec_a)
                & inside(up_a + out_a + a, sec_a) & inside(to_b, sec_b))
        key = jnp.where(live, (up_a * chans + i) * 3 + jnp.where(up_b == 0, q_b, 2), buckets)
        pack = (w_in * 2 + q_b) * 32 + (up_a + out_a + 1) * 8 + sp * 2 + to_b
        return key, key * (2 * wide) + q_b * wide + index, pack

    total = jnp.sum(held[:, 0:8, :], axis=0).astype(jnp.int32)
    lane = lax.broadcasted_iota(jnp.int32, (1, 128), 1)
    along = [keys(total[c:c + 1], lane + 128 * c, q)[1] for c in range(wide // 128) for q in (0, 1)]
    code = held[:, 8:8 + mine, :].reshape(wide, 128).astype(jnp.int32)
    value = held[:, 8 + mine:8 + 2 * mine, :].reshape(wide, 128)
    index = lax.broadcasted_iota(jnp.int32, (wide, 128), 0)
    lanes = lax.broadcasted_iota(jnp.int32, (wide, 128), 1)
    starts = jnp.zeros((1, 128), jnp.int32)
    packs = [jnp.zeros((1, 128), jnp.float32) for _ in range(2 * wide // 128)]
    values = [jnp.zeros((1, 128), jnp.float32) for _ in range(2 * wide // 128)]
    for q in (0, 1):
        key, order, pack = keys(code, index, q)
        starts += jnp.sum(jnp.where(key < lanes, 1.0, 0.0), axis=0, keepdims=True).astype(jnp.int32)
        before = jnp.zeros((wide, 128), jnp.float32)
        for other in along:
            before += jnp.where(other < order, 1.0, 0.0)
        rank = jnp.sum(before, axis=1, keepdims=True).astype(jnp.int32)
        pack = pack.astype(jnp.float32)
        for c in range(len(packs)):
            hit = rank == lanes + 128 * c
            packs[c] += jnp.sum(jnp.where(hit, pack, 0.0), axis=0, keepdims=True)
            values[c] += jnp.sum(jnp.where(hit, value, 0.0), axis=0, keepdims=True)
    for c in range(len(packs)):
        ints[c:c + 1, :] = packs[c].astype(jnp.int32)
        floats[c:c + 1, :] = values[c]
    ints[4:5, :] = starts


def gather_kernel(n, chans, sec_a, sec_b, sizes, env, bra_hbm, info, env_all, bra_all, info_all, ints, floats,
                  info_own, env_own, bra_raw, bra, send, recv, isend, irecv, bsend, brecv, local):
    a = lax.axis_index("sec")
    row = lax.axis_index("row")
    pos = ring_pos(row, n)
    half = n // 2
    right, left = (ring_row(lax.rem(pos + d, n), n) for d in (1, n - 1))
    blocks = chans * sec_b

    barrier = pltpu.get_barrier_semaphore()
    for other in (right, left):
        pl.semaphore_signal(barrier, inc=1, device_id={"row": other}, device_id_type=MESH)
    for d in (-2, -1, 1, 2):
        @pl.when((a + d >= 0) & (a + d < sec_a))
        def _(d=d):
            pl.semaphore_signal(barrier, inc=1, device_id={"sec": a + d}, device_id_type=MESH)
    count = 2 + jnp.minimum(a, 2) + jnp.minimum(sec_a - 1 - a, 2)
    pl.semaphore_wait(barrier, count)

    hops, masks, _ = hop_masks(n, chans, sec_b)

    def used(k, way, b):
        return k <= hops and any(masks[k - 1][way][b])

    def carried(k, way, b, source):
        low, inner, high = masks[k - 1][way][b]
        mask = jnp.where(a == 0, low, jnp.where(a == sec_a - 1, high, inner))
        return lax.rem(lax.shift_right_logical(mask, source), 2) == 1

    def source_at(k, way):
        return ring_row(lax.rem(pos + (n - k if way == 0 else k), n), n)

    def block_copy(k, way, b, source):
        src = env.at[b] if k == 1 else env_all.at[source * blocks + b]
        return pltpu.make_async_remote_copy(
            src_ref=src, dst_ref=env_all.at[source * blocks + b],
            send_sem=send.at[k - 1, way, b], recv_sem=recv.at[k - 1, way, b],
            device_id={"row": left if way else right}, device_id_type=MESH)

    def info_copy(k, way, source):
        src = info if k == 1 else info_all.at[source]
        return pltpu.make_async_remote_copy(
            src_ref=src, dst_ref=info_all.at[source],
            send_sem=isend.at[k - 1, way], recv_sem=irecv.at[k - 1, way],
            device_id={"row": left if way else right}, device_id_type=MESH)

    def info_used(k, way):
        return k < half or way == 0

    def bra_copies():
        made = []
        for j, (d, slot) in enumerate(((1, 0), (-1, 2), (-2, 3))):
            made.append((d, pltpu.make_async_remote_copy(
                src_ref=bra, dst_ref=bra_all.at[slot],
                send_sem=bsend.at[j], recv_sem=brecv.at[j],
                device_id={"sec": a + d}, device_id_type=MESH)))
        return made

    for way in (0, 1):
        info_copy(1, way, row).start()
    for at in range(blocks):
        for way in (0, 1):
            b = blocks - 1 - at if way else at
            if used(1, way, b):
                @pl.when(carried(1, way, b, row))
                def _(b=b, way=way):
                    block_copy(1, way, b, row).start()
    loads = (
        pltpu.make_async_copy(bra_hbm, bra_raw, local.at[0]),
        pltpu.make_async_copy(env, env_own, local.at[1]),
    )
    for copy in loads:
        copy.start()

    def size_at(x, y):
        inner = jnp.where((x >= 0) & (y >= 0), sizes[jnp.maximum(x, 0) * sec_b + max(y, 0)], 0)
        return inner

    loads[0].wait()
    at_row = lax.broadcasted_iota(jnp.int32, bra.shape[1:], 0)
    at_col = lax.broadcasted_iota(jnp.int32, bra.shape[1:], 1)
    for j in range(4 * sec_b):
        sp, y = j // sec_b, j % sec_b
        keep = (at_row < size_at(a - sp % 2, y - sp // 2)) & (at_col < size_at(a, y))
        block = jnp.where(keep, bra_raw[j].astype(jnp.float32), 0.0)
        bra[j] = block.T.astype(bra.dtype)
    for d, copy in bra_copies():
        @pl.when((a + d >= 0) & (a + d < sec_a))
        def _(copy=copy):
            copy.start()
    loads[1].wait()
    own = (
        pltpu.make_async_copy(env_own, env_all.at[pl.ds(row * blocks, blocks)], local.at[1]),
        pltpu.make_async_copy(bra, bra_all.at[1], local.at[0]),
    )
    for copy in own:
        copy.start()

    for k in range(1, hops + 1):
        sources = [source_at(k, way) for way in (0, 1)]
        for way in (0, 1):
            if k <= half and info_used(k, way):
                info_copy(k, way, sources[way]).wait_recv()
                if k < half and info_used(k + 1, way):
                    info_copy(k + 1, way, sources[way]).start()
        if k == half:
            fill_lists(n, chans, sec_a, sec_b, a, row, info, info_all, info_own, ints, floats, local.at[2])
        for at in range(blocks):
            for way in (0, 1):
                b = blocks - 1 - at if way else at
                if used(k, way, b):
                    @pl.when(carried(k, way, b, sources[way]))
                    def _(k=k, way=way, b=b):
                        block_copy(k, way, b, sources[way]).wait_recv()
                        if used(k + 1, way, b):
                            @pl.when(carried(k + 1, way, b, sources[way]))
                            def _():
                                block_copy(k + 1, way, b, sources[way]).start()

    for k in range(1, hops + 1):
        for way in (0, 1):
            source = row if k == 1 else source_at(k - 1, way)
            if k <= half and info_used(k, way):
                info_copy(k, way, source).wait_send()
            for b in range(blocks):
                if used(k, way, b):
                    @pl.when(carried(k, way, b, source))
                    def _(k=k, way=way, b=b, source=source):
                        block_copy(k, way, b, source).wait_send()
    for d, copy in bra_copies():
        @pl.when((a + d >= 0) & (a + d < sec_a))
        def _(copy=copy):
            copy.wait_send()

        @pl.when((a - d >= 0) & (a - d < sec_a))
        def _(copy=copy):
            copy.wait_recv()
    for copy in own:
        copy.wait()


def gather(sizes, env, bra, info, n, chans, sec_a, sec_b):
    half, blocks = n // 2, chans * sec_b
    hops = hop_masks(n, chans, sec_b)[0]
    anywhere = pl.BlockSpec(memory_space=pl.ANY)
    dma = pltpu.SemaphoreType.DMA
    return pl.pallas_call(
        functools.partial(gather_kernel, n, chans, sec_a, sec_b),
        out_shape=(
            jax.ShapeDtypeStruct((n * blocks,) + env.shape[1:], env.dtype),
            jax.ShapeDtypeStruct((4,) + bra.shape, bra.dtype),
            jax.ShapeDtypeStruct((n,) + info.shape, info.dtype),
            jax.ShapeDtypeStruct((8, 128), jnp.int32),
            jax.ShapeDtypeStruct((8, 128), jnp.float32),
        ),
        in_specs=[pl.BlockSpec(memory_space=pltpu.SMEM)] + [anywhere] * 3,
        out_specs=(anywhere,) * 3 + (pl.BlockSpec(memory_space=pltpu.VMEM),) * 2,
        scratch_shapes=[
            pltpu.VMEM((n,) + info.shape, info.dtype), pltpu.VMEM(env.shape, env.dtype), pltpu.VMEM(bra.shape, bra.dtype), pltpu.VMEM(bra.shape, bra.dtype),
            dma((hops, 2, blocks)), dma((hops, 2, blocks)), dma((half, 2)), dma((half, 2)),
            dma((3,)), dma((3,)), dma((3,)),
        ],
        compiler_params=pltpu.CompilerParams(
            collective_id=0, has_side_effects=True, vmem_limit_bytes=60 * 1024 * 1024),
        name="gather_row",
    )(sizes, env, bra, info)


def terms_kernel(up_a, base, count, sec_a, ints, floats, ksz, env, bra, ket, out,
                 buf, t_acc, acc, sems):
    a = lax.axis_index("sec")
    to_a = jnp.minimum(a + up_a, sec_a - 1)

    def at(j):
        return ints[lax.div(j, 128), lax.rem(j, 128)]

    def start(bucket):
        return ints[4, bucket]

    first, last = start(base * 3), start((base + count) * 3)

    def fetch(j):
        slot = lax.rem(j, DEPTH)
        return pltpu.make_async_copy(env.at[lax.div(at(j), 32)], buf.at[slot], sems.at[slot])

    for d in range(DEPTH):
        @pl.when(first + d < last)
        def _(d=d):
            fetch(first + d).start()

    acc[...] = jnp.zeros_like(acc)
    cols = lax.broadcasted_iota(jnp.int32, t_acc.shape, 1)

    def channel(i, carry):
        for kind, (up_b, q_b) in enumerate(((0, 0), (0, 1), (1, 0))):
            bucket = (base + i) * 3 + kind
            begin, end = start(bucket), start(bucket + 1)

            @pl.when(end > begin)
            def _():
                t_acc[...] = jnp.zeros_like(t_acc)

                def item(j, c):
                    fetch(j).wait()
                    b = bra[lax.rem(at(j), 32)]
                    e = buf[lax.rem(j, DEPTH)]
                    t_acc[...] += floats[lax.div(j, 128), lax.rem(j, 128)] * jnp.dot(b, e, preferred_element_type=jnp.float32)

                    @pl.when(j + DEPTH < last)
                    def _():
                        fetch(j + DEPTH).start()
                    return c

                lax.fori_loop(begin, end, item, 0)
                t = jnp.where(cols < ksz[a * 2 + q_b], t_acc[...], 0.0).astype(jnp.bfloat16)
                k = ket[(up_a + 2 * up_b) * 2 + q_b]
                acc[i * 2 + up_b + q_b] += jnp.dot(t, k, preferred_element_type=jnp.float32)
        for p_b in (0, 1):
            block = acc[i * 2 + p_b]
            out[i * 2 + p_b] = jnp.where(cols < ksz[to_a * 2 + p_b], block, 0.0).astype(out.dtype)
        return carry

    lax.fori_loop(0, count, channel, 0)


def terms(up_a, chans, at, count, sec_a, ints, floats, ksz, env, bra, ket, dtype):
    rows, cols = env.shape[1:]
    blocks = count * 2
    smem = pl.BlockSpec(memory_space=pltpu.SMEM)
    vmem = pl.BlockSpec(memory_space=pltpu.VMEM)
    return pl.pallas_call(
        functools.partial(terms_kernel, up_a, up_a * chans + at, count, sec_a),
        out_shape=jax.ShapeDtypeStruct((blocks, rows, cols), dtype),
        in_specs=[smem] * 3 + [pl.BlockSpec(memory_space=pl.ANY), vmem, vmem],
        out_specs=pl.BlockSpec(memory_space=pltpu.VMEM),
        scratch_shapes=[
            pltpu.VMEM((DEPTH, rows, cols), env.dtype),
            pltpu.VMEM((rows, cols), jnp.float32),
            pltpu.VMEM((blocks, rows, cols), jnp.float32),
            pltpu.SemaphoreType.DMA((DEPTH,)),
        ],
        compiler_params=pltpu.CompilerParams(vmem_limit_bytes=40 * 1024 * 1024),
        cost_estimate=pl.CostEstimate(flops=5 * 10**9, bytes_accessed=16 * 2**20, transcendentals=0),
        name="terms_up" if up_a else "terms_same",
    )(ints, floats, ksz, env, bra, ket)


def body(env_in, ket_mps, bra_mps, ket_sizes, bra_sizes, entries, coeffs):
    chans, _, sec_b, bra_w, ket_w = env_in.shape
    a = lax.axis_index("sec")
    row = lax.axis_index("row")
    sec_a, n = lax.axis_size("sec"), lax.axis_size("row")
    bra = bra_mps.reshape(4 * sec_b, bra_w, bra_w)
    mine, wide = chans * EPW, n * chans * EPW
    w_in = (row * chans + jnp.arange(chans, dtype=jnp.int32))[:, None]
    in_a, in_b = channel_charge(w_in)
    out_a, out_b = channel_charge(entries[..., 0])
    code = entries[..., 0] * 32 + w_in
    for field in (entries[..., 1], entries[..., 2], in_a + 1, in_b + 1, out_a + 1, out_b + 1):
        code = code * 4 + field
    code = code.reshape(-1).astype(jnp.float32)
    lanes = lax.dynamic_update_slice(jnp.zeros((wide,), jnp.float32), code, (row * mine,)).reshape(-1, 128)
    info = jnp.concatenate([
        jnp.pad(lanes, ((0, 8 - lanes.shape[0]), (0, 0))),
        jnp.broadcast_to(code[:, None], (mine, 128)),
        jnp.broadcast_to(coeffs.reshape(-1)[:, None], (mine, 128)),
    ])

    env_all, bra_all, _, ints, floats = gather(
        bra_sizes.reshape(-1), env_in.reshape(chans * sec_b, bra_w, ket_w), bra, info, n, chans, sec_a, sec_b)
    bra_all = bra_all.reshape(4 * 4 * sec_b, bra_w, bra_w)

    ket = ket_mps.reshape(4 * sec_b, ket_w, ket_w)
    ksz = ket_sizes.reshape(-1)
    sent = []
    part = chans // 2
    for at in (0, part):
        up = terms(1, chans, at, part, sec_a, ints, floats, ksz, env_all, bra_all, ket, jnp.bfloat16)
        sent.append(lax.ppermute(up, "sec", [(k, k + 1) for k in range(sec_a - 1)]))
    same = terms(0, chans, 0, chans, sec_a, ints, floats, ksz, env_all, bra_all, ket, jnp.float32)
    out = (same + jnp.concatenate(sent).astype(jnp.float32)).astype(env_in.dtype)
    return out.reshape(env_in.shape)


def solution(mesh):
    placed = (
        P("row", "sec", None, None, None),
        P(None, "sec", None, None, None),
        P(None, "sec", None, None, None),
        P(),
        P(),
        P("row", None, None),
        P("row", None),
    )
    return jax.shard_map(
        body,
        mesh=mesh,
        in_specs=placed,
        out_specs=P("row", "sec", None, None, None),
        check_vma=False,
    )
```

```python
import functools

import jax
import jax.numpy as jnp
from jax import lax
from jax.experimental import pallas as pl
from jax.experimental.pallas import tpu as pltpu
from jax.sharding import PartitionSpec as P

EPW = 8
Z = 4
DEPTH = 8
MESH = pl.DeviceIdType.MESH


def channel_charge(channel):
    klass = lax.rem(channel, 9)
    return lax.rem(klass, 3) - 1, lax.div(klass, 3) - 1


def ring_pos(row, n):
    wide = n // Z
    z, x = lax.div(row, wide), lax.rem(row, wide)
    t = jnp.where(lax.rem(z, 2) == 0, x - 1, wide - 1 - x)
    return jnp.where(x == 0, Z * (wide - 1) + Z - 1 - z, z * (wide - 1) + t)


def ring_row(pos, n):
    wide = n // Z
    z, t = lax.div(pos, wide - 1), lax.rem(pos, wide - 1)
    x = jnp.where(lax.rem(z, 2) == 0, 1 + t, wide - 1 - t)
    back = Z - 1 - (pos - Z * (wide - 1))
    return jnp.where(pos < Z * (wide - 1), z * wide + x, back * wide)


@functools.lru_cache(maxsize=None)
def hop_masks(n, chans, sec_b):
    wide, half, blocks = n // Z, n // 2, chans * sec_b
    order = [z * wide + (1 + t if z % 2 == 0 else wide - 1 - t) for z in range(Z) for t in range(wide - 1)]
    order += [z * wide for z in reversed(range(Z))]
    classes = {}
    shared = None
    for dead in (None, -1, 1):
        items = []
        for p, source in enumerate(order):
            for b in range(blocks):
                klass = (source * chans + b // sec_b) % 9
                to_b = klass // 3 - 1 + b % sec_b
                if 0 <= to_b < sec_b and klass % 3 - 1 != dead:
                    items.append((p, source, b))
        reach = {item: half - (item[2] * 2 >= blocks) for item in items}

        def links(item, d):
            p = item[0]
            return [(0, (p + t) % n) for t in range(d)] + [(1, (p - 1 - t) % n) for t in range(n - 1 - d)]

        load = dict(shared) if shared else {(way, j): 0 for way in (0, 1) for j in range(n)}
        for item in items:
            for link in links(item, reach[item]):
                load[link] += 1
        for _ in range(12):
            for item in items:
                for link in links(item, reach[item]):
                    load[link] -= 1
                costs = []
                for d in range(half - 2, half + 2):
                    extra = sum((load[link] + 1) ** 6 - load[link] ** 6 for link in links(item, d))
                    costs.append((extra, abs(2 * d - n + 1), d))
                reach[item] = min(costs)[2]
                for link in links(item, reach[item]):
                    load[link] += 1
        classes[dead] = (reach, max(load.values()))
        shared = shared or load
    classes = [classes[dead] for dead in (-1, None, 1)]
    hops = max(max(d, n - 1 - d) for reach, _ in classes for d in reach.values())
    masks = [[[[0, 0, 0] for _ in range(blocks)] for _ in (0, 1)] for _ in range(hops)]
    for c, (reach, _) in enumerate(classes):
        for (p, source, b), d in reach.items():
            for way, count in ((0, d), (1, n - 1 - d)):
                for k in range(count):
                    masks[k][way][b][c] |= 1 << source
    return hops, masks, [top for _, top in classes]


def fill_lists(n, chans, sec_a, sec_b, a, row, info, info_all, held, ints, floats, sem):
    for source in range(n):
        @pl.when(row == source)
        def _(source=source):
            copy = pltpu.make_async_copy(info, held.at[source], sem)
            copy.start()
            copy.wait()

        @pl.when(row != source)
        def _(source=source):
            copy = pltpu.make_async_copy(info_all.at[source], held.at[source], sem)
            copy.start()
            copy.wait()
    mine = chans * EPW
    wide = n * mine
    buckets = 2 * chans * 3

    def inside(x, count):
        return (x >= 0) & (x < count)

    def keys(code, index, q_b):
        def field(at, bits=2):
            return lax.shift_right_logical(code, at) & ((1 << bits) - 1)

        out_b, out_a, in_b, in_a = (field(2 * j) - 1 for j in range(4))
        s, sp, w_in, w_out = field(8), field(10), field(12, 5), field(17, 5)
        up_a, up_b = s & 1, lax.shift_right_logical(s, 1)
        i = w_out - row * chans
        to_b = up_b + out_b + q_b
        live = (inside(i, chans) & inside(up_b + q_b, sec_b) & inside(up_a + a, sec_a)
                & inside(in_b + q_b, sec_b) & inside(in_a + a, sec_a)
                & inside(up_a + out_a + a, sec_a) & inside(to_b, sec_b))
        key = jnp.where(live, (up_a * chans + i) * 3 + jnp.where(up_b == 0, q_b, 2), buckets)
        pack = (w_in * 2 + q_b) * 32 + (up_a + out_a + 1) * 8 + sp * 2 + to_b
        return key, key * (2 * wide) + q_b * wide + index, pack

    total = jnp.sum(held[:, 0:8, :], axis=0).astype(jnp.int32)
    lane = lax.broadcasted_iota(jnp.int32, (1, 128), 1)
    along = [keys(total[c:c + 1], lane + 128 * c, q)[1] for c in range(wide // 128) for q in (0, 1)]
    code = held[:, 8:8 + mine, :].reshape(wide, 128).astype(jnp.int32)
    value = held[:, 8 + mine:8 + 2 * mine, :].reshape(wide, 128)
    index = lax.broadcasted_iota(jnp.int32, (wide, 128), 0)
    lanes = lax.broadcasted_iota(jnp.int32, (wide, 128), 1)
    starts = jnp.zeros((1, 128), jnp.int32)
    packs = [jnp.zeros((1, 128), jnp.float32) for _ in range(2 * wide // 128)]
    values = [jnp.zeros((1, 128), jnp.float32) for _ in range(2 * wide // 128)]
    for q in (0, 1):
        key, order, pack = keys(code, index, q)
        starts += jnp.sum(jnp.where(key < lanes, 1.0, 0.0), axis=0, keepdims=True).astype(jnp.int32)
        before = jnp.zeros((wide, 128), jnp.float32)
        for other in along:
            before += jnp.where(other < order, 1.0, 0.0)
        rank = jnp.sum(before, axis=1, keepdims=True).astype(jnp.int32)
        pack = pack.astype(jnp.float32)
        for c in range(len(packs)):
            hit = rank == lanes + 128 * c
            packs[c] += jnp.sum(jnp.where(hit, pack, 0.0), axis=0, keepdims=True)
            values[c] += jnp.sum(jnp.where(hit, value, 0.0), axis=0, keepdims=True)
    for c in range(len(packs)):
        ints[c:c + 1, :] = packs[c].astype(jnp.int32)
        floats[c:c + 1, :] = values[c]
    ints[4:5, :] = starts


def gather_kernel(n, chans, sec_a, sec_b, sizes, env, bra_hbm, info, env_all, bra_all, info_all, ints, floats,
                  info_own, env_own, bra_raw, bra, send, recv, isend, irecv, bsend, brecv, local, go):
    a = lax.axis_index("sec")
    row = lax.axis_index("row")
    pos = ring_pos(row, n)
    half = n // 2
    right, left = (ring_row(lax.rem(pos + d, n), n) for d in (1, n - 1))
    blocks = chans * sec_b

    barrier = pltpu.get_barrier_semaphore()
    for other in (right, left):
        pl.semaphore_signal(barrier, inc=1, device_id={"row": other}, device_id_type=MESH)
    for d in (-2, -1, 1, 2):
        @pl.when((a + d >= 0) & (a + d < sec_a))
        def _(d=d):
            pl.semaphore_signal(barrier, inc=1, device_id={"sec": a + d}, device_id_type=MESH)
    count = 2 + jnp.minimum(a, 2) + jnp.minimum(sec_a - 1 - a, 2)
    pl.semaphore_wait(barrier, count)

    hops, masks, _ = hop_masks(n, chans, sec_b)

    def used(k, way, b):
        return k <= hops and any(masks[k - 1][way][b])

    def carried(k, way, b, source):
        low, inner, high = masks[k - 1][way][b]
        mask = jnp.where(a == 0, low, jnp.where(a == sec_a - 1, high, inner))
        return lax.rem(lax.shift_right_logical(mask, source), 2) == 1

    def source_at(k, way):
        return ring_row(lax.rem(pos + (n - k if way == 0 else k), n), n)

    def block_copy(k, way, b, source):
        src = env.at[b] if k == 1 else env_all.at[source * blocks + b]
        return pltpu.make_async_remote_copy(
            src_ref=src, dst_ref=env_all.at[source * blocks + b],
            send_sem=send.at[k - 1, way, b], recv_sem=recv.at[k - 1, way, b],
            device_id={"row": left if way else right}, device_id_type=MESH)

    def info_copy(k, way, source):
        src = info if k == 1 else info_all.at[source]
        return pltpu.make_async_remote_copy(
            src_ref=src, dst_ref=info_all.at[source],
            send_sem=isend.at[k - 1, way], recv_sem=irecv.at[k - 1, way],
            device_id={"row": left if way else right}, device_id_type=MESH)

    def info_used(k, way):
        return k < half or way == 0

    def bra_copies():
        made = []
        for j, (d, slot) in enumerate(((1, 0), (-1, 2), (-2, 3))):
            made.append((d, pltpu.make_async_remote_copy(
                src_ref=bra, dst_ref=bra_all.at[slot],
                send_sem=bsend.at[j], recv_sem=brecv.at[j],
                device_id={"sec": a + d}, device_id_type=MESH)))
        return made

    for way in (0, 1):
        info_copy(1, way, row).start()
    staged = sec_a >= 4

    def first_hop():
        for at in range(blocks):
            for way in (0, 1):
                b = blocks - 1 - at if way else at
                if used(1, way, b):
                    @pl.when(carried(1, way, b, row))
                    def _(b=b, way=way):
                        block_copy(1, way, b, row).start()

    if staged:
        pl.when((a > 0) & (a < sec_a - 1))(first_hop)
    else:
        first_hop()
    loads = (
        pltpu.make_async_copy(bra_hbm, bra_raw, local.at[0]),
        pltpu.make_async_copy(env, env_own, local.at[1]),
    )
    for copy in loads:
        copy.start()

    def size_at(x, y):
        inner = jnp.where((x >= 0) & (y >= 0), sizes[jnp.maximum(x, 0) * sec_b + max(y, 0)], 0)
        return inner

    loads[0].wait()
    at_row = lax.broadcasted_iota(jnp.int32, bra.shape[1:], 0)
    at_col = lax.broadcasted_iota(jnp.int32, bra.shape[1:], 1)
    for j in range(4 * sec_b):
        sp, y = j // sec_b, j % sec_b
        keep = (at_row < size_at(a - sp % 2, y - sp // 2)) & (at_col < size_at(a, y))
        block = jnp.where(keep, bra_raw[j].astype(jnp.float32), 0.0)
        bra[j] = block.T.astype(bra.dtype)
    for d, copy in bra_copies():
        @pl.when((a + d >= 0) & (a + d < sec_a))
        def _(copy=copy):
            copy.start()
    loads[1].wait()
    own = (
        pltpu.make_async_copy(env_own, env_all.at[pl.ds(row * blocks, blocks)], local.at[1]),
        pltpu.make_async_copy(bra, bra_all.at[1], local.at[0]),
    )
    for copy in own:
        copy.start()
    if staged:
        @pl.when((a == 0) | (a == sec_a - 1))
        def _():
            pl.semaphore_wait(go, 1)
            first_hop()

    for k in range(1, hops + 1):
        sources = [source_at(k, way) for way in (0, 1)]
        for way in (0, 1):
            if k <= half and info_used(k, way):
                info_copy(k, way, sources[way]).wait_recv()
                if k < half and info_used(k + 1, way):
                    info_copy(k + 1, way, sources[way]).start()
        if k == half:
            fill_lists(n, chans, sec_a, sec_b, a, row, info, info_all, info_own, ints, floats, local.at[2])
        for at in range(blocks):
            for way in (0, 1):
                b = blocks - 1 - at if way else at
                if used(k, way, b):
                    @pl.when(carried(k, way, b, sources[way]))
                    def _(k=k, way=way, b=b):
                        block_copy(k, way, b, sources[way]).wait_recv()
                        if used(k + 1, way, b):
                            @pl.when(carried(k + 1, way, b, sources[way]))
                            def _():
                                block_copy(k + 1, way, b, sources[way]).start()
        if staged and k == half // 2:
            for inner, edge in ((1, 0), (sec_a - 2, sec_a - 1)):
                @pl.when(a == inner)
                def _(edge=edge):
                    pl.semaphore_signal(go, inc=1, device_id={"sec": edge}, device_id_type=MESH)

    for k in range(1, hops + 1):
        for way in (0, 1):
            source = row if k == 1 else source_at(k - 1, way)
            if k <= half and info_used(k, way):
                info_copy(k, way, source).wait_send()
            for b in range(blocks):
                if used(k, way, b):
                    @pl.when(carried(k, way, b, source))
                    def _(k=k, way=way, b=b, source=source):
                        block_copy(k, way, b, source).wait_send()
    for d, copy in bra_copies():
        @pl.when((a + d >= 0) & (a + d < sec_a))
        def _(copy=copy):
            copy.wait_send()

        @pl.when((a - d >= 0) & (a - d < sec_a))
        def _(copy=copy):
            copy.wait_recv()
    for copy in own:
        copy.wait()


def gather(sizes, env, bra, info, n, chans, sec_a, sec_b):
    half, blocks = n // 2, chans * sec_b
    hops = hop_masks(n, chans, sec_b)[0]
    anywhere = pl.BlockSpec(memory_space=pl.ANY)
    dma = pltpu.SemaphoreType.DMA
    return pl.pallas_call(
        functools.partial(gather_kernel, n, chans, sec_a, sec_b),
        out_shape=(
            jax.ShapeDtypeStruct((n * blocks,) + env.shape[1:], env.dtype),
            jax.ShapeDtypeStruct((4,) + bra.shape, bra.dtype),
            jax.ShapeDtypeStruct((n,) + info.shape, info.dtype),
            jax.ShapeDtypeStruct((8, 128), jnp.int32),
            jax.ShapeDtypeStruct((8, 128), jnp.float32),
        ),
        in_specs=[pl.BlockSpec(memory_space=pltpu.SMEM)] + [anywhere] * 3,
        out_specs=(anywhere,) * 3 + (pl.BlockSpec(memory_space=pltpu.VMEM),) * 2,
        scratch_shapes=[
            pltpu.VMEM((n,) + info.shape, info.dtype), pltpu.VMEM(env.shape, env.dtype), pltpu.VMEM(bra.shape, bra.dtype), pltpu.VMEM(bra.shape, bra.dtype),
            dma((hops, 2, blocks)), dma((hops, 2, blocks)), dma((half, 2)), dma((half, 2)),
            dma((3,)), dma((3,)), dma((3,)), pltpu.SemaphoreType.REGULAR,
        ],
        compiler_params=pltpu.CompilerParams(
            collective_id=0, has_side_effects=True, vmem_limit_bytes=54 * 1024 * 1024),
        name="gather_row",
    )(sizes, env, bra, info)


def terms_kernel(up_a, base, count, sec_a, ints, floats, ksz, env, bra, ket, out,
                 buf, t_acc, acc, sems):
    a = lax.axis_index("sec")
    to_a = jnp.minimum(a + up_a, sec_a - 1)

    def at(j):
        return ints[lax.div(j, 128), lax.rem(j, 128)]

    def start(bucket):
        return ints[4, bucket]

    first, last = start(base * 3), start((base + count) * 3)

    def fetch(j):
        slot = lax.rem(j, DEPTH)
        return pltpu.make_async_copy(env.at[lax.div(at(j), 32)], buf.at[slot], sems.at[slot])

    for d in range(DEPTH):
        @pl.when(first + d < last)
        def _(d=d):
            fetch(first + d).start()

    acc[...] = jnp.zeros_like(acc)
    cols = lax.broadcasted_iota(jnp.int32, t_acc.shape, 1)

    def channel(i, carry):
        for kind, (up_b, q_b) in enumerate(((0, 0), (0, 1), (1, 0))):
            bucket = (base + i) * 3 + kind
            begin, end = start(bucket), start(bucket + 1)

            @pl.when(end > begin)
            def _():
                t_acc[...] = jnp.zeros_like(t_acc)

                def item(j, c):
                    fetch(j).wait()
                    b = bra[lax.rem(at(j), 32)]
                    e = buf[lax.rem(j, DEPTH)]
                    t_acc[...] += floats[lax.div(j, 128), lax.rem(j, 128)] * jnp.dot(b, e, preferred_element_type=jnp.float32)

                    @pl.when(j + DEPTH < last)
                    def _():
                        fetch(j + DEPTH).start()
                    return c

                lax.fori_loop(begin, end, item, 0)
                t = jnp.where(cols < ksz[a * 2 + q_b], t_acc[...], 0.0).astype(jnp.bfloat16)
                k = ket[(up_a + 2 * up_b) * 2 + q_b]
                acc[i * 2 + up_b + q_b] += jnp.dot(t, k, preferred_element_type=jnp.float32)
        for p_b in (0, 1):
            block = acc[i * 2 + p_b]
            out[i * 2 + p_b] = jnp.where(cols < ksz[to_a * 2 + p_b], block, 0.0).astype(out.dtype)
        return carry

    lax.fori_loop(0, count, channel, 0)


def terms(up_a, chans, at, count, sec_a, ints, floats, ksz, env, bra, ket, dtype):
    rows, cols = env.shape[1:]
    blocks = count * 2
    smem = pl.BlockSpec(memory_space=pltpu.SMEM)
    vmem = pl.BlockSpec(memory_space=pltpu.VMEM)
    return pl.pallas_call(
        functools.partial(terms_kernel, up_a, up_a * chans + at, count, sec_a),
        out_shape=jax.ShapeDtypeStruct((blocks, rows, cols), dtype),
        in_specs=[smem] * 3 + [pl.BlockSpec(memory_space=pl.ANY), vmem, vmem],
        out_specs=pl.BlockSpec(memory_space=pltpu.VMEM),
        scratch_shapes=[
            pltpu.VMEM((DEPTH, rows, cols), env.dtype),
            pltpu.VMEM((rows, cols), jnp.float32),
            pltpu.VMEM((blocks, rows, cols), jnp.float32),
            pltpu.SemaphoreType.DMA((DEPTH,)),
        ],
        compiler_params=pltpu.CompilerParams(vmem_limit_bytes=28 * 1024 * 1024),
        cost_estimate=pl.CostEstimate(flops=5 * 10**9, bytes_accessed=16 * 2**20, transcendentals=0),
        name="terms_up" if up_a else "terms_same",
    )(ints, floats, ksz, env, bra, ket)


def body(env_in, ket_mps, bra_mps, ket_sizes, bra_sizes, entries, coeffs):
    chans, _, sec_b, bra_w, ket_w = env_in.shape
    a = lax.axis_index("sec")
    row = lax.axis_index("row")
    sec_a, n = lax.axis_size("sec"), lax.axis_size("row")
    bra = bra_mps.reshape(4 * sec_b, bra_w, bra_w)
    mine, wide = chans * EPW, n * chans * EPW
    w_in = (row * chans + jnp.arange(chans, dtype=jnp.int32))[:, None]
    in_a, in_b = channel_charge(w_in)
    out_a, out_b = channel_charge(entries[..., 0])
    code = entries[..., 0] * 32 + w_in
    for field in (entries[..., 1], entries[..., 2], in_a + 1, in_b + 1, out_a + 1, out_b + 1):
        code = code * 4 + field
    code = code.reshape(-1).astype(jnp.float32)
    lanes = lax.dynamic_update_slice(jnp.zeros((wide,), jnp.float32), code, (row * mine,)).reshape(-1, 128)
    info = jnp.concatenate([
        jnp.pad(lanes, ((0, 8 - lanes.shape[0]), (0, 0))),
        jnp.broadcast_to(code[:, None], (mine, 128)),
        jnp.broadcast_to(coeffs.reshape(-1)[:, None], (mine, 128)),
    ])

    env_all, bra_all, _, ints, floats = gather(
        bra_sizes.reshape(-1), env_in.reshape(chans * sec_b, bra_w, ket_w), bra, info, n, chans, sec_a, sec_b)
    bra_all = bra_all.reshape(4 * 4 * sec_b, bra_w, bra_w)

    ket = ket_mps.reshape(4 * sec_b, ket_w, ket_w)
    ksz = ket_sizes.reshape(-1)
    up = terms(1, chans, 0, chans, sec_a, ints, floats, ksz, env_all, bra_all, ket, jnp.bfloat16)
    up = lax.ppermute(up, "sec", [(k, k + 1) for k in range(sec_a - 1)])
    same = terms(0, chans, 0, chans, sec_a, ints, floats, ksz, env_all, bra_all, ket, jnp.float32)
    out = (same + up.astype(jnp.float32)).astype(env_in.dtype)
    return out.reshape(env_in.shape)


def solution(mesh):
    placed = (
        P("row", "sec", None, None, None),
        P(None, "sec", None, None, None),
        P(None, "sec", None, None, None),
        P(),
        P(),
        P("row", None, None),
        P("row", None),
    )
    return jax.shard_map(
        body,
        mesh=mesh,
        in_specs=placed,
        out_specs=P("row", "sec", None, None, None),
        check_vma=False,
    )
```

```python
import functools

import jax
import jax.numpy as jnp
from jax import lax
from jax.experimental import pallas as pl
from jax.experimental.pallas import tpu as pltpu
from jax.sharding import PartitionSpec as P

EPW = 8
Z = 4
DEPTH = 8
MESH = pl.DeviceIdType.MESH


def channel_charge(channel):
    klass = lax.rem(channel, 9)
    return lax.rem(klass, 3) - 1, lax.div(klass, 3) - 1


def ring_pos(row, n):
    wide = n // Z
    z, x = lax.div(row, wide), lax.rem(row, wide)
    t = jnp.where(lax.rem(z, 2) == 0, x - 1, wide - 1 - x)
    return jnp.where(x == 0, Z * (wide - 1) + Z - 1 - z, z * (wide - 1) + t)


def ring_row(pos, n):
    wide = n // Z
    z, t = lax.div(pos, wide - 1), lax.rem(pos, wide - 1)
    x = jnp.where(lax.rem(z, 2) == 0, 1 + t, wide - 1 - t)
    back = Z - 1 - (pos - Z * (wide - 1))
    return jnp.where(pos < Z * (wide - 1), z * wide + x, back * wide)


@functools.lru_cache(maxsize=None)
def hop_masks(n, chans, sec_b):
    wide, half, blocks = n // Z, n // 2, chans * sec_b
    order = [z * wide + (1 + t if z % 2 == 0 else wide - 1 - t) for z in range(Z) for t in range(wide - 1)]
    order += [z * wide for z in reversed(range(Z))]
    classes = {}
    shared = None
    for dead in (None, -1, 1):
        items = []
        for p, source in enumerate(order):
            for b in range(blocks):
                klass = (source * chans + b // sec_b) % 9
                to_b = klass // 3 - 1 + b % sec_b
                if 0 <= to_b < sec_b and klass % 3 - 1 != dead:
                    items.append((p, source, b))
        reach = {item: half - (item[2] * 2 >= blocks) for item in items}

        def links(item, d):
            p = item[0]
            return [(0, (p + t) % n) for t in range(d)] + [(1, (p - 1 - t) % n) for t in range(n - 1 - d)]

        load = dict(shared) if shared else {(way, j): 0 for way in (0, 1) for j in range(n)}
        for item in items:
            for link in links(item, reach[item]):
                load[link] += 1
        for _ in range(12):
            for item in items:
                for link in links(item, reach[item]):
                    load[link] -= 1
                costs = []
                for d in range(half - 2, half + 2):
                    extra = sum((load[link] + 1) ** 6 - load[link] ** 6 for link in links(item, d))
                    costs.append((extra, abs(2 * d - n + 1), d))
                reach[item] = min(costs)[2]
                for link in links(item, reach[item]):
                    load[link] += 1
        classes[dead] = (reach, max(load.values()))
        shared = shared or load
    classes = [classes[dead] for dead in (-1, None, 1)]
    hops = max(max(d, n - 1 - d) for reach, _ in classes for d in reach.values())
    masks = [[[[0, 0, 0] for _ in range(blocks)] for _ in (0, 1)] for _ in range(hops)]
    for c, (reach, _) in enumerate(classes):
        for (p, source, b), d in reach.items():
            for way, count in ((0, d), (1, n - 1 - d)):
                for k in range(count):
                    masks[k][way][b][c] |= 1 << source
    return hops, masks, [top for _, top in classes]


def fill_lists(n, chans, sec_a, sec_b, a, row, info, info_all, held, ints, floats, sem):
    for source in range(n):
        @pl.when(row == source)
        def _(source=source):
            copy = pltpu.make_async_copy(info, held.at[source], sem)
            copy.start()
            copy.wait()

        @pl.when(row != source)
        def _(source=source):
            copy = pltpu.make_async_copy(info_all.at[source], held.at[source], sem)
            copy.start()
            copy.wait()
    mine = chans * EPW
    wide = n * mine
    buckets = 2 * chans * 3

    def inside(x, count):
        return (x >= 0) & (x < count)

    def keys(code, index, q_b):
        def field(at, bits=2):
            return lax.shift_right_logical(code, at) & ((1 << bits) - 1)

        out_b, out_a, in_b, in_a = (field(2 * j) - 1 for j in range(4))
        s, sp, w_in, w_out = field(8), field(10), field(12, 5), field(17, 5)
        up_a, up_b = s & 1, lax.shift_right_logical(s, 1)
        i = w_out - row * chans
        to_b = up_b + out_b + q_b
        live = (inside(i, chans) & inside(up_b + q_b, sec_b) & inside(up_a + a, sec_a)
                & inside(in_b + q_b, sec_b) & inside(in_a + a, sec_a)
                & inside(up_a + out_a + a, sec_a) & inside(to_b, sec_b))
        key = jnp.where(live, (up_a * chans + i) * 3 + jnp.where(up_b == 0, q_b, 2), buckets)
        pack = (w_in * 2 + q_b) * 32 + (up_a + out_a + 1) * 8 + sp * 2 + to_b
        return key, key * (2 * wide) + q_b * wide + index, pack

    total = jnp.sum(held[:, 0:8, :], axis=0).astype(jnp.int32)
    lane = lax.broadcasted_iota(jnp.int32, (1, 128), 1)
    along = [keys(total[c:c + 1], lane + 128 * c, q)[1] for c in range(wide // 128) for q in (0, 1)]
    code = held[:, 8:8 + mine, :].reshape(wide, 128).astype(jnp.int32)
    value = held[:, 8 + mine:8 + 2 * mine, :].reshape(wide, 128)
    index = lax.broadcasted_iota(jnp.int32, (wide, 128), 0)
    lanes = lax.broadcasted_iota(jnp.int32, (wide, 128), 1)
    starts = jnp.zeros((1, 128), jnp.int32)
    packs = [jnp.zeros((1, 128), jnp.float32) for _ in range(2 * wide // 128)]
    values = [jnp.zeros((1, 128), jnp.float32) for _ in range(2 * wide // 128)]
    for q in (0, 1):
        key, order, pack = keys(code, index, q)
        starts += jnp.sum(jnp.where(key < lanes, 1.0, 0.0), axis=0, keepdims=True).astype(jnp.int32)
        before = jnp.zeros((wide, 128), jnp.float32)
        for other in along:
            before += jnp.where(other < order, 1.0, 0.0)
        rank = jnp.sum(before, axis=1, keepdims=True).astype(jnp.int32)
        pack = pack.astype(jnp.float32)
        for c in range(len(packs)):
            hit = rank == lanes + 128 * c
            packs[c] += jnp.sum(jnp.where(hit, pack, 0.0), axis=0, keepdims=True)
            values[c] += jnp.sum(jnp.where(hit, value, 0.0), axis=0, keepdims=True)
    for c in range(len(packs)):
        ints[c:c + 1, :] = packs[c].astype(jnp.int32)
        floats[c:c + 1, :] = values[c]
    ints[4:5, :] = starts


def gather_kernel(n, chans, sec_a, sec_b, sizes, env, bra_hbm, info, env_all, bra_all, info_all, ints, floats,
                  info_own, env_own, bra_raw, bra, send, recv, isend, irecv, bsend, brecv, local, go):
    a = lax.axis_index("sec")
    row = lax.axis_index("row")
    pos = ring_pos(row, n)
    half = n // 2
    right, left = (ring_row(lax.rem(pos + d, n), n) for d in (1, n - 1))
    blocks = chans * sec_b

    barrier = pltpu.get_barrier_semaphore()
    for other in (right, left):
        pl.semaphore_signal(barrier, inc=1, device_id={"row": other}, device_id_type=MESH)
    for d in (-2, -1, 1, 2):
        @pl.when((a + d >= 0) & (a + d < sec_a))
        def _(d=d):
            pl.semaphore_signal(barrier, inc=1, device_id={"sec": a + d}, device_id_type=MESH)
    count = 2 + jnp.minimum(a, 2) + jnp.minimum(sec_a - 1 - a, 2)
    pl.semaphore_wait(barrier, count)

    hops, masks, _ = hop_masks(n, chans, sec_b)

    def used(k, way, b):
        return k <= hops and any(masks[k - 1][way][b])

    def carried(k, way, b, source):
        low, inner, high = masks[k - 1][way][b]
        mask = jnp.where(a == 0, low, jnp.where(a == sec_a - 1, high, inner))
        return lax.rem(lax.shift_right_logical(mask, source), 2) == 1

    def source_at(k, way):
        return ring_row(lax.rem(pos + (n - k if way == 0 else k), n), n)

    def block_copy(k, way, b, source):
        src = env.at[b] if k == 1 else env_all.at[source * blocks + b]
        return pltpu.make_async_remote_copy(
            src_ref=src, dst_ref=env_all.at[source * blocks + b],
            send_sem=send.at[k - 1, way, b], recv_sem=recv.at[k - 1, way, b],
            device_id={"row": left if way else right}, device_id_type=MESH)

    def info_copy(k, way, source):
        src = info if k == 1 else info_all.at[source]
        return pltpu.make_async_remote_copy(
            src_ref=src, dst_ref=info_all.at[source],
            send_sem=isend.at[k - 1, way], recv_sem=irecv.at[k - 1, way],
            device_id={"row": left if way else right}, device_id_type=MESH)

    def info_used(k, way):
        return k < half or way == 0

    def bra_copies():
        made = []
        for j, (d, slot) in enumerate(((1, 0), (-1, 2), (-2, 3))):
            made.append((d, pltpu.make_async_remote_copy(
                src_ref=bra, dst_ref=bra_all.at[slot],
                send_sem=bsend.at[j], recv_sem=brecv.at[j],
                device_id={"sec": a + d}, device_id_type=MESH)))
        return made

    for way in (0, 1):
        info_copy(1, way, row).start()
    staged = sec_a >= 4

    def first_hop():
        for at in range(blocks):
            for way in (0, 1):
                b = blocks - 1 - at if way else at
                if used(1, way, b):
                    @pl.when(carried(1, way, b, row))
                    def _(b=b, way=way):
                        block_copy(1, way, b, row).start()

    if staged:
        pl.when((a > 0) & (a < sec_a - 1))(first_hop)
    else:
        first_hop()
    loads = (
        pltpu.make_async_copy(bra_hbm, bra_raw, local.at[0]),
        pltpu.make_async_copy(env, env_own, local.at[1]),
    )
    for copy in loads:
        copy.start()

    def size_at(x, y):
        inner = jnp.where((x >= 0) & (y >= 0), sizes[jnp.maximum(x, 0) * sec_b + max(y, 0)], 0)
        return inner

    loads[0].wait()
    at_row = lax.broadcasted_iota(jnp.int32, bra.shape[1:], 0)
    at_col = lax.broadcasted_iota(jnp.int32, bra.shape[1:], 1)
    for j in range(4 * sec_b):
        sp, y = j // sec_b, j % sec_b
        keep = (at_row < size_at(a - sp % 2, y - sp // 2)) & (at_col < size_at(a, y))
        block = jnp.where(keep, bra_raw[j].astype(jnp.float32), 0.0)
        bra[j] = block.T.astype(bra.dtype)
    for d, copy in bra_copies():
        @pl.when((a + d >= 0) & (a + d < sec_a))
        def _(copy=copy):
            copy.start()
    loads[1].wait()
    own = (
        pltpu.make_async_copy(env_own, env_all.at[pl.ds(row * blocks, blocks)], local.at[1]),
        pltpu.make_async_copy(bra, bra_all.at[1], local.at[0]),
    )
    for copy in own:
        copy.start()
    if staged:
        @pl.when((a == 0) | (a == sec_a - 1))
        def _():
            pl.semaphore_wait(go, 1)
            first_hop()

    for k in range(1, hops + 1):
        sources = [source_at(k, way) for way in (0, 1)]
        for way in (0, 1):
            if k <= half and info_used(k, way):
                info_copy(k, way, sources[way]).wait_recv()
                if k < half and info_used(k + 1, way):
                    info_copy(k + 1, way, sources[way]).start()
        if k == half:
            fill_lists(n, chans, sec_a, sec_b, a, row, info, info_all, info_own, ints, floats, local.at[2])
        for at in range(blocks):
            for way in (0, 1):
                b = blocks - 1 - at if way else at
                if used(k, way, b):
                    @pl.when(carried(k, way, b, sources[way]))
                    def _(k=k, way=way, b=b):
                        block_copy(k, way, b, sources[way]).wait_recv()
                        if used(k + 1, way, b):
                            @pl.when(carried(k + 1, way, b, sources[way]))
                            def _():
                                block_copy(k + 1, way, b, sources[way]).start()
        if staged and k == 1:
            for inner, edge in ((1, 0), (sec_a - 2, sec_a - 1)):
                @pl.when(a == inner)
                def _(edge=edge):
                    pl.semaphore_signal(go, inc=1, device_id={"sec": edge}, device_id_type=MESH)

    for k in range(1, hops + 1):
        for way in (0, 1):
            source = row if k == 1 else source_at(k - 1, way)
            if k <= half and info_used(k, way):
                info_copy(k, way, source).wait_send()
            for b in range(blocks):
                if used(k, way, b):
                    @pl.when(carried(k, way, b, source))
                    def _(k=k, way=way, b=b, source=source):
                        block_copy(k, way, b, source).wait_send()
    for d, copy in bra_copies():
        @pl.when((a + d >= 0) & (a + d < sec_a))
        def _(copy=copy):
            copy.wait_send()

        @pl.when((a - d >= 0) & (a - d < sec_a))
        def _(copy=copy):
            copy.wait_recv()
    for copy in own:
        copy.wait()


def gather(sizes, env, bra, info, n, chans, sec_a, sec_b):
    half, blocks = n // 2, chans * sec_b
    hops = hop_masks(n, chans, sec_b)[0]
    anywhere = pl.BlockSpec(memory_space=pl.ANY)
    dma = pltpu.SemaphoreType.DMA
    return pl.pallas_call(
        functools.partial(gather_kernel, n, chans, sec_a, sec_b),
        out_shape=(
            jax.ShapeDtypeStruct((n * blocks,) + env.shape[1:], env.dtype),
            jax.ShapeDtypeStruct((4,) + bra.shape, bra.dtype),
            jax.ShapeDtypeStruct((n,) + info.shape, info.dtype),
            jax.ShapeDtypeStruct((8, 128), jnp.int32),
            jax.ShapeDtypeStruct((8, 128), jnp.float32),
        ),
        in_specs=[pl.BlockSpec(memory_space=pltpu.SMEM)] + [anywhere] * 3,
        out_specs=(anywhere,) * 3 + (pl.BlockSpec(memory_space=pltpu.VMEM),) * 2,
        scratch_shapes=[
            pltpu.VMEM((n,) + info.shape, info.dtype), pltpu.VMEM(env.shape, env.dtype), pltpu.VMEM(bra.shape, bra.dtype), pltpu.VMEM(bra.shape, bra.dtype),
            dma((hops, 2, blocks)), dma((hops, 2, blocks)), dma((half, 2)), dma((half, 2)),
            dma((3,)), dma((3,)), dma((3,)), pltpu.SemaphoreType.REGULAR,
        ],
        compiler_params=pltpu.CompilerParams(
            collective_id=0, has_side_effects=True, vmem_limit_bytes=54 * 1024 * 1024),
        name="gather_row",
    )(sizes, env, bra, info)


def terms_kernel(up_a, base, count, sec_a, ints, floats, ksz, env, bra, ket, out,
                 buf, t_acc, acc, sems):
    a = lax.axis_index("sec")
    to_a = jnp.minimum(a + up_a, sec_a - 1)

    def at(j):
        return ints[lax.div(j, 128), lax.rem(j, 128)]

    def start(bucket):
        return ints[4, bucket]

    first, last = start(base * 3), start((base + count) * 3)

    def fetch(j):
        slot = lax.rem(j, DEPTH)
        return pltpu.make_async_copy(env.at[lax.div(at(j), 32)], buf.at[slot], sems.at[slot])

    for d in range(DEPTH):
        @pl.when(first + d < last)
        def _(d=d):
            fetch(first + d).start()

    acc[...] = jnp.zeros_like(acc)
    cols = lax.broadcasted_iota(jnp.int32, t_acc.shape, 1)

    def channel(i, carry):
        for kind, (up_b, q_b) in enumerate(((0, 0), (0, 1), (1, 0))):
            bucket = (base + i) * 3 + kind
            begin, end = start(bucket), start(bucket + 1)

            @pl.when(end > begin)
            def _():
                t_acc[...] = jnp.zeros_like(t_acc)

                def item(j, c):
                    fetch(j).wait()
                    b = bra[lax.rem(at(j), 32)]
                    e = buf[lax.rem(j, DEPTH)]
                    t_acc[...] += floats[lax.div(j, 128), lax.rem(j, 128)] * jnp.dot(b, e, preferred_element_type=jnp.float32)

                    @pl.when(j + DEPTH < last)
                    def _():
                        fetch(j + DEPTH).start()
                    return c

                lax.fori_loop(begin, end, item, 0)
                t = jnp.where(cols < ksz[a * 2 + q_b], t_acc[...], 0.0).astype(jnp.bfloat16)
                k = ket[(up_a + 2 * up_b) * 2 + q_b]
                acc[i * 2 + up_b + q_b] += jnp.dot(t, k, preferred_element_type=jnp.float32)
        for p_b in (0, 1):
            block = acc[i * 2 + p_b]
            out[i * 2 + p_b] = jnp.where(cols < ksz[to_a * 2 + p_b], block, 0.0).astype(out.dtype)
        return carry

    lax.fori_loop(0, count, channel, 0)


def terms(up_a, chans, at, count, sec_a, ints, floats, ksz, env, bra, ket, dtype):
    rows, cols = env.shape[1:]
    blocks = count * 2
    smem = pl.BlockSpec(memory_space=pltpu.SMEM)
    vmem = pl.BlockSpec(memory_space=pltpu.VMEM)
    return pl.pallas_call(
        functools.partial(terms_kernel, up_a, up_a * chans + at, count, sec_a),
        out_shape=jax.ShapeDtypeStruct((blocks, rows, cols), dtype),
        in_specs=[smem] * 3 + [pl.BlockSpec(memory_space=pl.ANY), vmem, vmem],
        out_specs=pl.BlockSpec(memory_space=pltpu.VMEM),
        scratch_shapes=[
            pltpu.VMEM((DEPTH, rows, cols), env.dtype),
            pltpu.VMEM((rows, cols), jnp.float32),
            pltpu.VMEM((blocks, rows, cols), jnp.float32),
            pltpu.SemaphoreType.DMA((DEPTH,)),
        ],
        compiler_params=pltpu.CompilerParams(vmem_limit_bytes=28 * 1024 * 1024),
        cost_estimate=pl.CostEstimate(flops=5 * 10**9, bytes_accessed=16 * 2**20, transcendentals=0),
        name="terms_up" if up_a else "terms_same",
    )(ints, floats, ksz, env, bra, ket)


def body(env_in, ket_mps, bra_mps, ket_sizes, bra_sizes, entries, coeffs):
    chans, _, sec_b, bra_w, ket_w = env_in.shape
    a = lax.axis_index("sec")
    row = lax.axis_index("row")
    sec_a, n = lax.axis_size("sec"), lax.axis_size("row")
    bra = bra_mps.reshape(4 * sec_b, bra_w, bra_w)
    mine, wide = chans * EPW, n * chans * EPW
    w_in = (row * chans + jnp.arange(chans, dtype=jnp.int32))[:, None]
    in_a, in_b = channel_charge(w_in)
    out_a, out_b = channel_charge(entries[..., 0])
    code = entries[..., 0] * 32 + w_in
    for field in (entries[..., 1], entries[..., 2], in_a + 1, in_b + 1, out_a + 1, out_b + 1):
        code = code * 4 + field
    code = code.reshape(-1).astype(jnp.float32)
    lanes = lax.dynamic_update_slice(jnp.zeros((wide,), jnp.float32), code, (row * mine,)).reshape(-1, 128)
    info = jnp.concatenate([
        jnp.pad(lanes, ((0, 8 - lanes.shape[0]), (0, 0))),
        jnp.broadcast_to(code[:, None], (mine, 128)),
        jnp.broadcast_to(coeffs.reshape(-1)[:, None], (mine, 128)),
    ])

    env_all, bra_all, _, ints, floats = gather(
        bra_sizes.reshape(-1), env_in.reshape(chans * sec_b, bra_w, ket_w), bra, info, n, chans, sec_a, sec_b)
    bra_all = bra_all.reshape(4 * 4 * sec_b, bra_w, bra_w)

    ket = ket_mps.reshape(4 * sec_b, ket_w, ket_w)
    ksz = ket_sizes.reshape(-1)
    up = terms(1, chans, 0, chans, sec_a, ints, floats, ksz, env_all, bra_all, ket, jnp.bfloat16)
    up = lax.ppermute(up, "sec", [(k, k + 1) for k in range(sec_a - 1)])
    same = terms(0, chans, 0, chans, sec_a, ints, floats, ksz, env_all, bra_all, ket, jnp.float32)
    out = (same + up.astype(jnp.float32)).astype(env_in.dtype)
    return out.reshape(env_in.shape)


def solution(mesh):
    placed = (
        P("row", "sec", None, None, None),
        P(None, "sec", None, None, None),
        P(None, "sec", None, None, None),
        P(),
        P(),
        P("row", None, None),
        P("row", None),
    )
    return jax.shard_map(
        body,
        mesh=mesh,
        in_specs=placed,
        out_specs=P("row", "sec", None, None, None),
        check_vma=False,
    )
```

```python
import functools

import jax
import jax.numpy as jnp
from jax import lax
from jax.experimental import pallas as pl
from jax.experimental.pallas import tpu as pltpu
from jax.sharding import PartitionSpec as P

EPW = 8
Z = 4
DEPTH = 8
MESH = pl.DeviceIdType.MESH


def channel_charge(channel):
    klass = lax.rem(channel, 9)
    return lax.rem(klass, 3) - 1, lax.div(klass, 3) - 1


def ring_pos(row, n):
    wide = n // Z
    z, x = lax.div(row, wide), lax.rem(row, wide)
    t = jnp.where(lax.rem(z, 2) == 0, x - 1, wide - 1 - x)
    return jnp.where(x == 0, Z * (wide - 1) + Z - 1 - z, z * (wide - 1) + t)


def ring_row(pos, n):
    wide = n // Z
    z, t = lax.div(pos, wide - 1), lax.rem(pos, wide - 1)
    x = jnp.where(lax.rem(z, 2) == 0, 1 + t, wide - 1 - t)
    back = Z - 1 - (pos - Z * (wide - 1))
    return jnp.where(pos < Z * (wide - 1), z * wide + x, back * wide)


@functools.lru_cache(maxsize=None)
def hop_masks(n, chans, sec_b):
    wide, half, blocks = n // Z, n // 2, chans * sec_b
    order = [z * wide + (1 + t if z % 2 == 0 else wide - 1 - t) for z in range(Z) for t in range(wide - 1)]
    order += [z * wide for z in reversed(range(Z))]
    classes = {}
    shared = None
    for dead in (None, -1, 1):
        items = []
        for p, source in enumerate(order):
            for b in range(blocks):
                klass = (source * chans + b // sec_b) % 9
                to_b = klass // 3 - 1 + b % sec_b
                if 0 <= to_b < sec_b and klass % 3 - 1 != dead:
                    items.append((p, source, b))
        reach = {item: half - (item[2] * 2 >= blocks) for item in items}

        def links(item, d):
            p = item[0]
            return [(0, (p + t) % n) for t in range(d)] + [(1, (p - 1 - t) % n) for t in range(n - 1 - d)]

        load = dict(shared) if shared else {(way, j): 0 for way in (0, 1) for j in range(n)}
        for item in items:
            for link in links(item, reach[item]):
                load[link] += 1
        for _ in range(12):
            for item in items:
                for link in links(item, reach[item]):
                    load[link] -= 1
                costs = []
                for d in range(half - 2, half + 2):
                    extra = sum((load[link] + 1) ** 6 - load[link] ** 6 for link in links(item, d))
                    costs.append((extra, abs(2 * d - n + 1), d))
                reach[item] = min(costs)[2]
                for link in links(item, reach[item]):
                    load[link] += 1
        classes[dead] = (reach, max(load.values()))
        shared = shared or load
    classes = [classes[dead] for dead in (-1, None, 1)]
    hops = max(max(d, n - 1 - d) for reach, _ in classes for d in reach.values())
    masks = [[[[0, 0, 0] for _ in range(blocks)] for _ in (0, 1)] for _ in range(hops)]
    for c, (reach, _) in enumerate(classes):
        for (p, source, b), d in reach.items():
            for way, count in ((0, d), (1, n - 1 - d)):
                for k in range(count):
                    masks[k][way][b][c] |= 1 << source
    return hops, masks, [top for _, top in classes]


def fill_lists(n, chans, sec_a, sec_b, a, row, info, info_all, held, ints, floats, sem):
    for source in range(n):
        @pl.when(row == source)
        def _(source=source):
            copy = pltpu.make_async_copy(info, held.at[source], sem)
            copy.start()
            copy.wait()

        @pl.when(row != source)
        def _(source=source):
            copy = pltpu.make_async_copy(info_all.at[source], held.at[source], sem)
            copy.start()
            copy.wait()
    mine = chans * EPW
    wide = n * mine
    buckets = 2 * chans * 3

    def inside(x, count):
        return (x >= 0) & (x < count)

    def keys(code, index, q_b):
        def field(at, bits=2):
            return lax.shift_right_logical(code, at) & ((1 << bits) - 1)

        out_b, out_a, in_b, in_a = (field(2 * j) - 1 for j in range(4))
        s, sp, w_in, w_out = field(8), field(10), field(12, 5), field(17, 5)
        up_a, up_b = s & 1, lax.shift_right_logical(s, 1)
        i = w_out - row * chans
        to_b = up_b + out_b + q_b
        live = (inside(i, chans) & inside(up_b + q_b, sec_b) & inside(up_a + a, sec_a)
                & inside(in_b + q_b, sec_b) & inside(in_a + a, sec_a)
                & inside(up_a + out_a + a, sec_a) & inside(to_b, sec_b))
        key = jnp.where(live, (up_a * chans + i) * 3 + jnp.where(up_b == 0, q_b, 2), buckets)
        pack = (w_in * 2 + q_b) * 32 + (up_a + out_a + 1) * 8 + sp * 2 + to_b
        return key, key * (2 * wide) + q_b * wide + index, pack

    total = jnp.sum(held[:, 0:8, :], axis=0).astype(jnp.int32)
    lane = lax.broadcasted_iota(jnp.int32, (1, 128), 1)
    along = [keys(total[c:c + 1], lane + 128 * c, q)[1] for c in range(wide // 128) for q in (0, 1)]
    code = held[:, 8:8 + mine, :].reshape(wide, 128).astype(jnp.int32)
    value = held[:, 8 + mine:8 + 2 * mine, :].reshape(wide, 128)
    index = lax.broadcasted_iota(jnp.int32, (wide, 128), 0)
    lanes = lax.broadcasted_iota(jnp.int32, (wide, 128), 1)
    starts = jnp.zeros((1, 128), jnp.int32)
    packs = [jnp.zeros((1, 128), jnp.float32) for _ in range(2 * wide // 128)]
    values = [jnp.zeros((1, 128), jnp.float32) for _ in range(2 * wide // 128)]
    for q in (0, 1):
        key, order, pack = keys(code, index, q)
        starts += jnp.sum(jnp.where(key < lanes, 1.0, 0.0), axis=0, keepdims=True).astype(jnp.int32)
        before = jnp.zeros((wide, 128), jnp.float32)
        for other in along:
            before += jnp.where(other < order, 1.0, 0.0)
        rank = jnp.sum(before, axis=1, keepdims=True).astype(jnp.int32)
        pack = pack.astype(jnp.float32)
        for c in range(len(packs)):
            hit = rank == lanes + 128 * c
            packs[c] += jnp.sum(jnp.where(hit, pack, 0.0), axis=0, keepdims=True)
            values[c] += jnp.sum(jnp.where(hit, value, 0.0), axis=0, keepdims=True)
    for c in range(len(packs)):
        ints[c:c + 1, :] = packs[c].astype(jnp.int32)
        floats[c:c + 1, :] = values[c]
    ints[4:5, :] = starts


def gather_kernel(n, chans, sec_a, sec_b, sizes, env, bra_hbm, info, env_all, bra_all, info_all, ints, floats,
                  info_own, env_own, bra_raw, bra, send, recv, isend, irecv, bsend, brecv, local, go):
    a = lax.axis_index("sec")
    row = lax.axis_index("row")
    pos = ring_pos(row, n)
    half = n // 2
    right, left = (ring_row(lax.rem(pos + d, n), n) for d in (1, n - 1))
    blocks = chans * sec_b

    barrier = pltpu.get_barrier_semaphore()
    for other in (right, left):
        pl.semaphore_signal(barrier, inc=1, device_id={"row": other}, device_id_type=MESH)
    for d in (-2, -1, 1, 2):
        @pl.when((a + d >= 0) & (a + d < sec_a))
        def _(d=d):
            pl.semaphore_signal(barrier, inc=1, device_id={"sec": a + d}, device_id_type=MESH)
    count = 2 + jnp.minimum(a, 2) + jnp.minimum(sec_a - 1 - a, 2)
    pl.semaphore_wait(barrier, count)

    hops, masks, _ = hop_masks(n, chans, sec_b)

    def used(k, way, b):
        return k <= hops and any(masks[k - 1][way][b])

    def carried(k, way, b, source):
        low, inner, high = masks[k - 1][way][b]
        mask = jnp.where(a == 0, low, jnp.where(a == sec_a - 1, high, inner))
        return lax.rem(lax.shift_right_logical(mask, source), 2) == 1

    def source_at(k, way):
        return ring_row(lax.rem(pos + (n - k if way == 0 else k), n), n)

    def block_copy(k, way, b, source):
        src = env.at[b] if k == 1 else env_all.at[source * blocks + b]
        return pltpu.make_async_remote_copy(
            src_ref=src, dst_ref=env_all.at[source * blocks + b],
            send_sem=send.at[k - 1, way, b], recv_sem=recv.at[k - 1, way, b],
            device_id={"row": left if way else right}, device_id_type=MESH)

    def info_copy(k, way, source):
        src = info if k == 1 else info_all.at[source]
        return pltpu.make_async_remote_copy(
            src_ref=src, dst_ref=info_all.at[source],
            send_sem=isend.at[k - 1, way], recv_sem=irecv.at[k - 1, way],
            device_id={"row": left if way else right}, device_id_type=MESH)

    def info_used(k, way):
        return k < half or way == 0

    def bra_copies():
        made = []
        for j, (d, slot) in enumerate(((1, 0), (-1, 2), (-2, 3))):
            made.append((d, pltpu.make_async_remote_copy(
                src_ref=bra, dst_ref=bra_all.at[slot],
                send_sem=bsend.at[j], recv_sem=brecv.at[j],
                device_id={"sec": a + d}, device_id_type=MESH)))
        return made

    for way in (0, 1):
        info_copy(1, way, row).start()
    staged = sec_a >= 4

    def first_hop():
        for at in range(blocks):
            for way in (0, 1):
                b = blocks - 1 - at if way else at
                if used(1, way, b):
                    @pl.when(carried(1, way, b, row))
                    def _(b=b, way=way):
                        block_copy(1, way, b, row).start()

    if staged:
        pl.when((a > 0) & (a < sec_a - 1))(first_hop)
    else:
        first_hop()
    loads = (
        pltpu.make_async_copy(bra_hbm, bra_raw, local.at[0]),
        pltpu.make_async_copy(env, env_own, local.at[1]),
    )
    for copy in loads:
        copy.start()

    def size_at(x, y):
        inner = jnp.where((x >= 0) & (y >= 0), sizes[jnp.maximum(x, 0) * sec_b + max(y, 0)], 0)
        return inner

    loads[0].wait()
    at_row = lax.broadcasted_iota(jnp.int32, bra.shape[1:], 0)
    at_col = lax.broadcasted_iota(jnp.int32, bra.shape[1:], 1)
    for j in range(4 * sec_b):
        sp, y = j // sec_b, j % sec_b
        keep = (at_row < size_at(a - sp % 2, y - sp // 2)) & (at_col < size_at(a, y))
        block = jnp.where(keep, bra_raw[j].astype(jnp.float32), 0.0)
        bra[j] = block.T.astype(bra.dtype)
    for d, copy in bra_copies():
        @pl.when((a + d >= 0) & (a + d < sec_a))
        def _(copy=copy):
            copy.start()
    loads[1].wait()
    own = (
        pltpu.make_async_copy(env_own, env_all.at[pl.ds(row * blocks, blocks)], local.at[1]),
        pltpu.make_async_copy(bra, bra_all.at[1], local.at[0]),
    )
    for copy in own:
        copy.start()
    if staged:
        @pl.when((a == 0) | (a == sec_a - 1))
        def _():
            pl.semaphore_wait(go, 1)
            first_hop()

    for k in range(1, hops + 1):
        sources = [source_at(k, way) for way in (0, 1)]
        for way in (0, 1):
            if k <= half and info_used(k, way):
                info_copy(k, way, sources[way]).wait_recv()
                if k < half and info_used(k + 1, way):
                    info_copy(k + 1, way, sources[way]).start()
        if k == half:
            fill_lists(n, chans, sec_a, sec_b, a, row, info, info_all, info_own, ints, floats, local.at[2])
        for at in range(blocks):
            for way in (0, 1):
                b = blocks - 1 - at if way else at
                if used(k, way, b):
                    @pl.when(carried(k, way, b, sources[way]))
                    def _(k=k, way=way, b=b):
                        block_copy(k, way, b, sources[way]).wait_recv()
                        if used(k + 1, way, b):
                            @pl.when(carried(k + 1, way, b, sources[way]))
                            def _():
                                block_copy(k + 1, way, b, sources[way]).start()
        if staged and k == half // 2 + 1:
            for inner, edge in ((1, 0), (sec_a - 2, sec_a - 1)):
                @pl.when(a == inner)
                def _(edge=edge):
                    pl.semaphore_signal(go, inc=1, device_id={"sec": edge}, device_id_type=MESH)

    for k in range(1, hops + 1):
        for way in (0, 1):
            source = row if k == 1 else source_at(k - 1, way)
            if k <= half and info_used(k, way):
                info_copy(k, way, source).wait_send()
            for b in range(blocks):
                if used(k, way, b):
                    @pl.when(carried(k, way, b, source))
                    def _(k=k, way=way, b=b, source=source):
                        block_copy(k, way, b, source).wait_send()
    for d, copy in bra_copies():
        @pl.when((a + d >= 0) & (a + d < sec_a))
        def _(copy=copy):
            copy.wait_send()

        @pl.when((a - d >= 0) & (a - d < sec_a))
        def _(copy=copy):
            copy.wait_recv()
    for copy in own:
        copy.wait()


def gather(sizes, env, bra, info, n, chans, sec_a, sec_b):
    half, blocks = n // 2, chans * sec_b
    hops = hop_masks(n, chans, sec_b)[0]
    anywhere = pl.BlockSpec(memory_space=pl.ANY)
    dma = pltpu.SemaphoreType.DMA
    return pl.pallas_call(
        functools.partial(gather_kernel, n, chans, sec_a, sec_b),
        out_shape=(
            jax.ShapeDtypeStruct((n * blocks,) + env.shape[1:], env.dtype),
            jax.ShapeDtypeStruct((4,) + bra.shape, bra.dtype),
            jax.ShapeDtypeStruct((n,) + info.shape, info.dtype),
            jax.ShapeDtypeStruct((8, 128), jnp.int32),
            jax.ShapeDtypeStruct((8, 128), jnp.float32),
        ),
        in_specs=[pl.BlockSpec(memory_space=pltpu.SMEM)] + [anywhere] * 3,
        out_specs=(anywhere,) * 3 + (pl.BlockSpec(memory_space=pltpu.VMEM),) * 2,
        scratch_shapes=[
            pltpu.VMEM((n,) + info.shape, info.dtype), pltpu.VMEM(env.shape, env.dtype), pltpu.VMEM(bra.shape, bra.dtype), pltpu.VMEM(bra.shape, bra.dtype),
            dma((hops, 2, blocks)), dma((hops, 2, blocks)), dma((half, 2)), dma((half, 2)),
            dma((3,)), dma((3,)), dma((3,)), pltpu.SemaphoreType.REGULAR,
        ],
        compiler_params=pltpu.CompilerParams(
            collective_id=0, has_side_effects=True, vmem_limit_bytes=54 * 1024 * 1024),
        name="gather_row",
    )(sizes, env, bra, info)


def terms_kernel(up_a, base, count, sec_a, ints, floats, ksz, env, bra, ket, out,
                 buf, t_acc, acc, sems):
    a = lax.axis_index("sec")
    to_a = jnp.minimum(a + up_a, sec_a - 1)

    def at(j):
        return ints[lax.div(j, 128), lax.rem(j, 128)]

    def start(bucket):
        return ints[4, bucket]

    first, last = start(base * 3), start((base + count) * 3)

    def fetch(j):
        slot = lax.rem(j, DEPTH)
        return pltpu.make_async_copy(env.at[lax.div(at(j), 32)], buf.at[slot], sems.at[slot])

    for d in range(DEPTH):
        @pl.when(first + d < last)
        def _(d=d):
            fetch(first + d).start()

    acc[...] = jnp.zeros_like(acc)
    cols = lax.broadcasted_iota(jnp.int32, t_acc.shape, 1)

    def channel(i, carry):
        for kind, (up_b, q_b) in enumerate(((0, 0), (0, 1), (1, 0))):
            bucket = (base + i) * 3 + kind
            begin, end = start(bucket), start(bucket + 1)

            @pl.when(end > begin)
            def _():
                t_acc[...] = jnp.zeros_like(t_acc)

                def item(j, c):
                    fetch(j).wait()
                    b = bra[lax.rem(at(j), 32)]
                    e = buf[lax.rem(j, DEPTH)]
                    t_acc[...] += floats[lax.div(j, 128), lax.rem(j, 128)] * jnp.dot(b, e, preferred_element_type=jnp.float32)

                    @pl.when(j + DEPTH < last)
                    def _():
                        fetch(j + DEPTH).start()
                    return c

                lax.fori_loop(begin, end, item, 0)
                t = jnp.where(cols < ksz[a * 2 + q_b], t_acc[...], 0.0).astype(jnp.bfloat16)
                k = ket[(up_a + 2 * up_b) * 2 + q_b]
                acc[i * 2 + up_b + q_b] += jnp.dot(t, k, preferred_element_type=jnp.float32)
        for p_b in (0, 1):
            block = acc[i * 2 + p_b]
            out[i * 2 + p_b] = jnp.where(cols < ksz[to_a * 2 + p_b], block, 0.0).astype(out.dtype)
        return carry

    lax.fori_loop(0, count, channel, 0)


def terms(up_a, chans, at, count, sec_a, ints, floats, ksz, env, bra, ket, dtype):
    rows, cols = env.shape[1:]
    blocks = count * 2
    smem = pl.BlockSpec(memory_space=pltpu.SMEM)
    vmem = pl.BlockSpec(memory_space=pltpu.VMEM)
    return pl.pallas_call(
        functools.partial(terms_kernel, up_a, up_a * chans + at, count, sec_a),
        out_shape=jax.ShapeDtypeStruct((blocks, rows, cols), dtype),
        in_specs=[smem] * 3 + [pl.BlockSpec(memory_space=pl.ANY), vmem, vmem],
        out_specs=pl.BlockSpec(memory_space=pltpu.VMEM),
        scratch_shapes=[
            pltpu.VMEM((DEPTH, rows, cols), env.dtype),
            pltpu.VMEM((rows, cols), jnp.float32),
            pltpu.VMEM((blocks, rows, cols), jnp.float32),
            pltpu.SemaphoreType.DMA((DEPTH,)),
        ],
        compiler_params=pltpu.CompilerParams(vmem_limit_bytes=28 * 1024 * 1024),
        cost_estimate=pl.CostEstimate(flops=5 * 10**9, bytes_accessed=16 * 2**20, transcendentals=0),
        name="terms_up" if up_a else "terms_same",
    )(ints, floats, ksz, env, bra, ket)


def body(env_in, ket_mps, bra_mps, ket_sizes, bra_sizes, entries, coeffs):
    chans, _, sec_b, bra_w, ket_w = env_in.shape
    a = lax.axis_index("sec")
    row = lax.axis_index("row")
    sec_a, n = lax.axis_size("sec"), lax.axis_size("row")
    bra = bra_mps.reshape(4 * sec_b, bra_w, bra_w)
    mine, wide = chans * EPW, n * chans * EPW
    w_in = (row * chans + jnp.arange(chans, dtype=jnp.int32))[:, None]
    in_a, in_b = channel_charge(w_in)
    out_a, out_b = channel_charge(entries[..., 0])
    code = entries[..., 0] * 32 + w_in
    for field in (entries[..., 1], entries[..., 2], in_a + 1, in_b + 1, out_a + 1, out_b + 1):
        code = code * 4 + field
    code = code.reshape(-1).astype(jnp.float32)
    lanes = lax.dynamic_update_slice(jnp.zeros((wide,), jnp.float32), code, (row * mine,)).reshape(-1, 128)
    info = jnp.concatenate([
        jnp.pad(lanes, ((0, 8 - lanes.shape[0]), (0, 0))),
        jnp.broadcast_to(code[:, None], (mine, 128)),
        jnp.broadcast_to(coeffs.reshape(-1)[:, None], (mine, 128)),
    ])

    env_all, bra_all, _, ints, floats = gather(
        bra_sizes.reshape(-1), env_in.reshape(chans * sec_b, bra_w, ket_w), bra, info, n, chans, sec_a, sec_b)
    bra_all = bra_all.reshape(4 * 4 * sec_b, bra_w, bra_w)

    ket = ket_mps.reshape(4 * sec_b, ket_w, ket_w)
    ksz = ket_sizes.reshape(-1)
    up = terms(1, chans, 0, chans, sec_a, ints, floats, ksz, env_all, bra_all, ket, jnp.bfloat16)
    up = lax.ppermute(up, "sec", [(k, k + 1) for k in range(sec_a - 1)])
    same = terms(0, chans, 0, chans, sec_a, ints, floats, ksz, env_all, bra_all, ket, jnp.float32)
    out = (same + up.astype(jnp.float32)).astype(env_in.dtype)
    return out.reshape(env_in.shape)


def solution(mesh):
    placed = (
        P("row", "sec", None, None, None),
        P(None, "sec", None, None, None),
        P(None, "sec", None, None, None),
        P(),
        P(),
        P("row", None, None),
        P("row", None),
    )
    return jax.shard_map(
        body,
        mesh=mesh,
        in_specs=placed,
        out_specs=P("row", "sec", None, None, None),
        check_vma=False,
    )
```
